32 devices in a mesh: dp: 8 (over z, y), tp: 4 (over x, core).
Axes of the slice: x: 2, y: 2, z: 4, core: 2. Of those that a mesh axis runs over, the one named last changes fastest.
Arguments:
- queries: bfloat16 [2, 8, 8192], P(None, 'dp', 'tp'), may hold values from -8 to 8
- new_token_keys: bfloat16 [2, 8, 512], P(None, 'dp', 'tp'), may hold values from -6 to 6
- new_token_values: bfloat16 [2, 8, 512], P(None, 'dp', 'tp'), may hold values from -6 to 6
- key_pool: bfloat16 [512, 128, 512], P('dp', None, 'tp'), may hold values from -8 to 8
- value_pool: bfloat16 [512, 128, 512], P('dp', None, 'tp'), may hold values from -6 to 6
- block_list: int32 [2, 256, 2], P(None, ('dp', 'tp')), may hold values from 0 to 63, as said below
- context_len: int32 [2, 8], P(None, 'dp'), may hold values from 1 to 4096, as said below
Outputs:
- attn_out: bfloat16 [2, 8, 8192], P(None, 'dp', 'tp')
The draws below stay inside these ranges and needn't reach their ends.
Inputs may be any that keep to these rules, and one draw needn't show every extreme that they name: `block_list`: each entry is (holder rank, pool slot). Every slot of every holder holds exactly one block of one micro-batch. On one holder, the blocks of one rank's requests over both micro-batches number 0 or 8; the bound 8 is also reached within a single micro-batch. Cached tokens, the new token aside. For every rank and micro-batch, ceil(context_len / 128) summed over the rank's 1 request is 32.
All inputs are finite; a program needn't handle non-finite values.
Results may differ from the reference program's by a relative error of at most 0.011.
Values may be sent and summed in bfloat16 or wider, within the bound.
A program may use at most 64 MiB of HBM per device.

```python
import math
import jax
import jax.numpy as jnp
from jax import lax

QUERY_HEADS = 64
KEY_VALUE_HEADS = 4
HEAD_SIZE = 128
BLOCK_TOKENS = 128
SLOTS = 64
MICRO_BATCHES = 2
RANK_REQUESTS = 1
BATCH_REQUESTS = 8
POOL_SLOTS = 512
N_DP = 8


def layout(key):
    per_rank = SLOTS // 2
    capacity = max(2, SLOTS // N_DP)
    groups = SLOTS // capacity
    row_total = MICRO_BATCHES * N_DP
    cut_key, tail_key, pick_key, group_key, offset_key, order_key = jax.random.split(key, 6)

    def cuts_for(row_key):
        points = jnp.sort(jax.random.permutation(row_key, per_rank - 1)[:RANK_REQUESTS - 1] + 1).astype(jnp.int32)
        boundary = jnp.concatenate([jnp.zeros((1,), jnp.int32), points, jnp.full((1,), per_rank, jnp.int32)])
        return boundary[1:] - boundary[:-1]
    counts = jax.vmap(cuts_for)(jax.random.split(cut_key, row_total))
    tail_tokens = jax.random.randint(tail_key, (row_total, RANK_REQUESTS), 1, BLOCK_TOKENS + 1)
    chosen = jax.random.randint(pick_key, (), 0, row_total)
    forced = (jnp.arange(row_total, dtype=jnp.int32) == chosen)[:, None]
    leading = (jnp.arange(RANK_REQUESTS, dtype=jnp.int32) == 0)[None, :]
    counts = jnp.where(forced, jnp.where(leading, per_rank - RANK_REQUESTS + 1, 1), counts)
    tail_tokens = jnp.where(forced, jnp.where(leading, BLOCK_TOKENS, 1), tail_tokens)
    lengths = ((counts - 1) * BLOCK_TOKENS + tail_tokens).astype(jnp.int32)
    slot_group = jax.random.permutation(group_key, SLOTS) // capacity
    shuffled = jax.random.permutation(offset_key, N_DP).astype(jnp.int32)
    rank_of = jnp.argsort(shuffled, stable=True).astype(jnp.int32)
    candidates = jnp.arange(N_DP, dtype=jnp.int32)
    score = jnp.where(candidates == 1, -2, jnp.where(candidates == N_DP // 2, -1, rank_of))
    offsets = jnp.argsort(score, stable=True).astype(jnp.int32)[:groups]
    slot_offset = offsets[slot_group]

    def order_for(row_key):
        rank_key, pair_key = jax.random.split(row_key)
        ranking = jax.random.permutation(rank_key, SLOTS)
        pair_groups = jax.random.permutation(pair_key, groups)[:2]
        tier_rank = jnp.where(slot_group == pair_groups[0], 0, jnp.where(slot_group == pair_groups[1], 2, 1))
        return jnp.argsort(tier_rank * SLOTS + ranking, stable=True).astype(jnp.int32)
    orders = jax.vmap(order_for)(jax.random.split(order_key, N_DP))
    holders = (jnp.arange(N_DP, dtype=jnp.int32)[:, None] + slot_offset[orders]) % N_DP
    slot_ids = jnp.transpose(orders.reshape(N_DP, MICRO_BATCHES, per_rank), (1, 0, 2))
    holder_ids = jnp.transpose(holders.reshape(N_DP, MICRO_BATCHES, per_rank), (1, 0, 2))
    block_list = jnp.stack([holder_ids, slot_ids], axis=-1).reshape(MICRO_BATCHES, N_DP * per_rank, 2).astype(jnp.int32)
    return (block_list, lengths.reshape(MICRO_BATCHES, N_DP * RANK_REQUESTS))


def draw_block_list(key, part):
    tables = layout(key)
    return tables[0]


def draw_context_len(key, part):
    tables = layout(key)
    return tables[1]


def draw_queries(key, part):
    key = jax.random.fold_in(key, 1)
    random_seed_key = jax.random.fold_in(key, 1)
    value_entries = jax.random.normal(random_seed_key, (MICRO_BATCHES, BATCH_REQUESTS, QUERY_HEADS, HEAD_SIZE))
    return jnp.clip(value_entries, -8.0, 8.0).reshape(MICRO_BATCHES, BATCH_REQUESTS, QUERY_HEADS * HEAD_SIZE).astype(jnp.bfloat16)


def draw_key_pool(key, part):
    key = jax.random.fold_in(key, 2)
    random_seed_key = jax.random.fold_in(key, 1)
    value_entries = jax.random.normal(random_seed_key, (POOL_SLOTS, BLOCK_TOKENS, KEY_VALUE_HEADS, HEAD_SIZE))
    return jnp.clip(value_entries, -8.0, 8.0).reshape(POOL_SLOTS, BLOCK_TOKENS, KEY_VALUE_HEADS * HEAD_SIZE).astype(jnp.bfloat16)


def steps_of(rng, extent, cuts, low, top_value):
    loudness, own = 1.0, jax.random.fold_in(rng, 6)
    for axis_at, blocks in cuts:
        steps = jnp.exp(jax.random.uniform(jax.random.fold_in(own, axis_at), (blocks,), jnp.float32, low / len(cuts), top_value / len(cuts)))
        loudness = loudness * jnp.repeat(steps, extent[axis_at] // blocks).reshape([-1 if axis == axis_at else 1 for axis in range(len(extent))])
    return loudness


def gaussian(own_key, dims, width, limit, cuts=(), kind=jnp.bfloat16):
    array = jax.random.normal(own_key, dims, jnp.float32) * width
    if len(cuts) > 0:
        array = steps_of(own_key, dims, cuts, -0.22, 0.18) * array
    return jnp.clip(array, min=-limit, max=limit).astype(kind)


def setup_inputs(seed: int = 0) -> dict:
    keys = jax.random.split(jax.random.key(seed), 8)
    return {
        "queries": draw_queries(jax.random.fold_in(keys[7], 71), 0),
        "new_token_keys": gaussian(keys[1], (MICRO_BATCHES, BATCH_REQUESTS, KEY_VALUE_HEADS * HEAD_SIZE), 1.0, 6.0, ((1, 8), (2, 4))),
        "new_token_values": gaussian(keys[2], (MICRO_BATCHES, BATCH_REQUESTS, KEY_VALUE_HEADS * HEAD_SIZE), 1.0, 6.0, ((1, 8), (2, 4))),
        "key_pool": draw_key_pool(jax.random.fold_in(keys[7], 71), 0),
        "value_pool": gaussian(keys[4], (POOL_SLOTS, BLOCK_TOKENS, KEY_VALUE_HEADS * HEAD_SIZE), 1.0, 6.0, ((0, 8), (2, 4))),
        "block_list": draw_block_list(jax.random.fold_in(keys[7], 71), 0),
        "context_len": draw_context_len(jax.random.fold_in(keys[7], 71), 0),
    }


def block_terms(query_row_list, key_row_list, value_row_list, live_tokens):
    score_scale = query_row_list.shape[-1] ** -0.5
    scores = jnp.einsum("ekgd,ebkd->ekgb", query_row_list.astype(jnp.float32), key_row_list.astype(jnp.float32), precision=lax.Precision.HIGHEST) * score_scale
    live_mask = lax.broadcasted_iota(jnp.int32, scores.shape, 3) < live_tokens[:, None, None, None]
    scores = jnp.where(live_mask, scores, -1e30)
    peak_score = jnp.max(scores, axis=3)
    weight = jnp.where(live_mask, jnp.exp(scores - peak_score[..., None]), 0.0)
    weight_sum = jnp.sum(weight, axis=3)
    rounded = lax.optimization_barrier(weight.astype(jnp.bfloat16)).astype(jnp.float32)
    mixed_sum = jnp.einsum("ekgb,ebkd->ekgd", rounded, value_row_list.astype(jnp.float32), precision=lax.Precision.HIGHEST)
    partial_value = (mixed_sum / weight_sum[..., None]).astype(jnp.bfloat16)
    return partial_value, peak_score, weight_sum


def micro_batch(query_tile_block, fresh_key, fresh_value, key_pool, value_pool, block_rows, lengths):
    request_count, feature_width = query_tile_block.shape
    owner_ranks = request_count // RANK_REQUESTS
    per_rank = SLOTS // 2
    heads_per_group = QUERY_HEADS // KEY_VALUE_HEADS
    score_scale = HEAD_SIZE ** -0.5
    lengths = lengths.reshape(owner_ranks, RANK_REQUESTS)
    block_counts = (lengths + BLOCK_TOKENS - 1) // BLOCK_TOKENS
    block_ends = jnp.cumsum(block_counts, axis=1)
    block_starts = block_ends - block_counts
    position = jnp.arange(per_rank, dtype=jnp.int32)
    request = jnp.sum((position[None, :, None] >= block_ends[:, None, :]).astype(jnp.int32), axis=2)
    chosen = request[:, :, None] == jnp.arange(RANK_REQUESTS, dtype=jnp.int32)[None, None, :]
    first_block = jnp.sum(jnp.where(chosen, block_starts[:, None, :], 0), axis=2)
    span_tokens = jnp.sum(jnp.where(chosen, lengths[:, None, :], 0), axis=2)
    live_tokens = jnp.clip(span_tokens - (position[None, :] - first_block) * BLOCK_TOKENS, 0, BLOCK_TOKENS).reshape(-1).astype(jnp.int32)
    pool_rows = (block_rows[:, 0] * SLOTS + block_rows[:, 1]).astype(jnp.int32)
    query_ids = (jnp.arange(owner_ranks, dtype=jnp.int32)[:, None] * RANK_REQUESTS + request).reshape(-1).astype(jnp.int32)
    entries = owner_ranks * per_rank
    batch_rows = math.gcd(entries, 64)

    def one_batch(pieces):
        query_portion, pool_portion, token_piece = pieces
        query_row_list = jnp.take(query_tile_block, query_portion, axis=0).reshape(batch_rows, KEY_VALUE_HEADS, heads_per_group, HEAD_SIZE)
        key_row_list = jnp.take(key_pool, pool_portion, axis=0).reshape(batch_rows, BLOCK_TOKENS, KEY_VALUE_HEADS, HEAD_SIZE)
        value_row_list = jnp.take(value_pool, pool_portion, axis=0).reshape(batch_rows, BLOCK_TOKENS, KEY_VALUE_HEADS, HEAD_SIZE)
        return block_terms(query_row_list, key_row_list, value_row_list, token_piece)

    partial_value, peak_score, weight_sum = lax.map(one_batch, (query_ids.reshape(-1, batch_rows), pool_rows.reshape(-1, batch_rows), live_tokens.reshape(-1, batch_rows)))
    partial_value = partial_value.reshape(owner_ranks, per_rank, QUERY_HEADS, HEAD_SIZE)
    peak_score = peak_score.reshape(owner_ranks, per_rank, QUERY_HEADS)
    weight_sum = weight_sum.reshape(owner_ranks, per_rank, QUERY_HEADS)
    query_head_rows = query_tile_block.reshape(owner_ranks, RANK_REQUESTS, KEY_VALUE_HEADS, heads_per_group, HEAD_SIZE).astype(jnp.float32)
    key_head_rows = fresh_key.reshape(owner_ranks, RANK_REQUESTS, KEY_VALUE_HEADS, HEAD_SIZE).astype(jnp.float32)
    own_score = jnp.einsum("orkgd,orkd->orkg", query_head_rows, key_head_rows, precision=lax.Precision.HIGHEST).reshape(owner_ranks, RANK_REQUESTS, QUERY_HEADS) * score_scale
    member = jnp.transpose(chosen, (0, 2, 1))[..., None]
    ceiling = jnp.maximum(own_score, jnp.max(jnp.where(member, peak_score[:, None], -1e30), axis=2))
    block_weight = jnp.where(member, jnp.exp(peak_score[:, None] - ceiling[:, :, None]) * weight_sum[:, None], 0.0)
    self_weight = jnp.exp(own_score - ceiling)
    value_head_rows = jnp.repeat(fresh_value.reshape(owner_ranks, RANK_REQUESTS, KEY_VALUE_HEADS, HEAD_SIZE), heads_per_group, axis=2).astype(jnp.float32)
    numerator = jnp.einsum("orbh,obhd->orhd", block_weight, partial_value.astype(jnp.float32), precision=lax.Precision.HIGHEST) + self_weight[..., None] * value_head_rows
    denominator = jnp.sum(block_weight, axis=2) + self_weight
    return (numerator / denominator[..., None]).astype(jnp.bfloat16).reshape(request_count, feature_width)


def reference(queries, new_token_keys, new_token_values, key_pool, value_pool, block_list, context_len):
    outputs = [micro_batch(queries[index], new_token_keys[index], new_token_values[index], key_pool, value_pool, block_list[index], context_len[index]) for index in range(queries.shape[0])]
    return jnp.stack(outputs)
```

```python
from functools import partial

import jax
import jax.numpy as jnp
from jax import lax
from jax.experimental import pallas as pl
from jax.experimental.pallas import tpu as pltpu
from jax.sharding import PartitionSpec as P

F32, BF16 = jnp.float32, jnp.bfloat16
LOW = -1e30
LANES = 128
RANK_CHUNK = 8
ROLLED_FROM = 64


def each(count, body):
    if count < ROLLED_FROM:
        for index in range(count):
            body(index)
    else:
        pl.loop(0, count)(body)


def iota(shape, axis):
    return lax.broadcasted_iota(jnp.int32, shape, axis)


def matmul(a, b):
    return jnp.dot(a, b, preferred_element_type=F32)


def kernel(
    ranks, shards, micro, heads,
    meta_ref, q_ref, new_k_ref, new_v_ref, k_hbm, v_hbm, out_ref,
    meta_all, q_all, k_vm, v_vm, pick, held, q_sel, scores, ceil_rep, acc_out, stat_out,
    acc_in, stat_in, kv_sem, send_sem, recv_sem,
):
    devices = ranks * shards
    slots, tokens, dim = k_vm.shape
    rows = micro * heads
    tall = slots * heads
    chunk_rows = RANK_CHUNK * rows
    chunks = ranks // RANK_CHUNK
    scale = dim ** (-0.5)
    rank, shard = lax.axis_index("dp"), lax.axis_index("tp")
    me = rank * shards + shard

    load_k = pltpu.make_async_copy(k_hbm, k_vm, kv_sem.at[0])
    load_v = pltpu.make_async_copy(v_hbm, v_vm, kv_sem.at[1])
    load_k.start()
    load_v.start()

    def device_at(step):
        other = lax.rem(me + step + 1, devices)
        return (other // shards, lax.rem(other, shards))

    def rank_at(step):
        return lax.rem(rank + step + 1, ranks)

    barrier = pltpu.get_barrier_semaphore()

    def greet(step):
        pl.semaphore_signal(
            barrier, inc=1, device_id=device_at(step), device_id_type=pl.DeviceIdType.MESH
        )

    each(devices - 1, greet)
    meta_all[me] = meta_ref[...]
    q_all[rank] = q_ref[...]
    pl.semaphore_wait(barrier, devices - 1)

    def send(src, dst, which, target):
        pltpu.make_async_remote_copy(
            src_ref=src, dst_ref=dst, send_sem=send_sem.at[which], recv_sem=recv_sem.at[which],
            device_id=target, device_id_type=pl.DeviceIdType.MESH,
        ).start()

    def drain(ref, sem, which, count):
        part = ref.at[pl.ds(0, count)]
        pltpu.make_async_copy(part, part, sem.at[which]).wait()

    each(devices - 1, lambda i: send(meta_all.at[me], meta_all.at[me], 0, device_at(i)))
    each(ranks - 1, lambda i: send(q_all.at[rank], q_all.at[rank], 1, (rank_at(i), shard)))

    lane = iota((1, LANES), 1)
    row_lane = lax.rem(iota((rows, LANES), 1), rows) == iota((rows, LANES), 0)
    spread = (iota((tall, slots), 0) // heads == iota((tall, slots), 1)).astype(F32).astype(BF16)
    spread_t = iota((slots, tall), 1) // heads == iota((slots, tall), 0)
    ones = jnp.ones((LANES, LANES), BF16)

    def per_head(ref):
        return jnp.concatenate(
            [jnp.broadcast_to(ref[m : m + 1, :].astype(F32), (heads, dim)) for m in range(micro)], 0
        )

    own = jnp.sum(q_ref[...].astype(F32) * per_head(new_k_ref), axis=1, keepdims=True) * scale
    own_row = jnp.sum(jnp.where(row_lane, own, 0.0), axis=0, keepdims=True)

    drain(meta_all, recv_sem, 0, devices - 1)
    entries = LANES // RANK_CHUNK
    slot_row = (rank * slots + iota((slots, LANES), 0)).astype(F32)
    half = entries // micro

    def find(group, carry):
        request, live = carry
        parts = meta_all[pl.ds(group * RANK_CHUNK, RANK_CHUNK)]
        both = jnp.sum(parts, axis=0)
        owner = (group * RANK_CHUNK + lane // entries) // shards
        name = (owner * micro + lax.rem(lane, entries) // half).astype(F32)
        match = jnp.broadcast_to(both[0:1], (slots, LANES)) == slot_row
        request = request + jnp.where(match, name, 0.0)
        live = live + jnp.where(match, both[1:2], 0.0)
        return request, live

    found = (jnp.zeros((slots, LANES), F32), jnp.zeros((slots, LANES), F32))
    groups = devices // RANK_CHUNK
    if groups < 16:
        for group in range(groups):
            found = find(group, found)
    else:
        found = lax.fori_loop(0, groups, find, found)
    summed = matmul(jnp.concatenate(found, axis=0).astype(BF16), ones)
    request = summed[:slots]
    wide = matmul(
        spread, jnp.concatenate([request, summed[slots:]], axis=1).astype(BF16)
    )
    request_tall, live_tall = wide[:, :LANES], wide[:, LANES:]
    target = request_tall * heads + lax.rem(iota((tall, LANES), 0), heads).astype(F32)
    target_row = jnp.sum(
        jnp.where(spread_t, jnp.concatenate([request] * (tall // LANES), axis=1), 0.0),
        axis=0, keepdims=True,
    ) * heads + lax.rem(iota((1, tall), 1), heads).astype(F32)

    def choose(c):
        for at in range(0, chunk_rows, LANES):
            column = (c * chunk_rows + at + iota((tall, LANES), 1)).astype(F32)
            pick[c, :, at : at + LANES] = jnp.where(target == column, 1.0, 0.0).astype(BF16)
        held[c] = jnp.where(
            (c * chunk_rows + iota((chunk_rows, tall), 0)).astype(F32) == target_row, 1.0, 0.0
        ).astype(BF16)

    each_chunk = lambda body: body(0) if chunks == 1 else pl.loop(0, chunks)(body)
    each_chunk(choose)

    drain(q_all, recv_sem, 1, ranks - 1)
    if chunks == 1:
        q_sel[...] = matmul(pick[0], q_all[...].reshape(chunk_rows, dim))
    else:
        q_sel[...] = jnp.zeros((tall, dim), F32)

        @pl.loop(0, chunks)
        def _(c):
            part = q_all[pl.ds(c * RANK_CHUNK, RANK_CHUNK)].reshape(chunk_rows, dim)
            q_sel[...] += matmul(pick[c], part)

    load_k.wait()
    batched = (((2,), (2,)), ((0,), (0,)))
    raw = lax.dot_general(
        q_sel[...].astype(BF16).reshape(slots, heads, dim), k_vm[...], batched,
        preferred_element_type=F32,
    ).reshape(tall, tokens) * scale
    alive = iota((tall, tokens), 1).astype(F32) < live_tall
    raw = jnp.where(alive, raw, LOW)
    scores[...] = raw
    peak = jnp.max(raw, axis=1, keepdims=True)

    def ceilings(c):
        name = (c * RANK_CHUNK * micro + iota((tall, LANES), 1)).astype(F32)
        best = jnp.where(request_tall == name, peak, LOW).reshape(slots, heads, LANES)
        best = jnp.max(best, axis=0).astype(BF16).astype(F32)
        top = jnp.concatenate(
            [
                jnp.broadcast_to(best[:, r : r + 1], (heads, LANES))
                for r in range(RANK_CHUNK * micro)
            ], 0,
        )
        stat_rows(c, 0, top)
        return top.astype(BF16)

    lane_slot = lax.rem(rank, LANES // rows) * rows

    def stat_rows(c, which, values):
        mine = iota((rows, LANES), 1) == iota((rows, LANES), 0) + lane_slot
        for o in range(RANK_CHUNK):
            part = jnp.where(mine, values[o * rows : (o + 1) * rows], 0.0)
            stat_out[c * RANK_CHUNK + o, which : which + 1] = jnp.sum(part, axis=0, keepdims=True)

    if chunks == 1:
        ceil_rep[...] = matmul(pick[0], ceilings(0))
    else:
        ceil_rep[...] = jnp.zeros((tall, LANES), F32)

        @pl.loop(0, chunks)
        def _(c):
            ceil_rep[...] += matmul(pick[c], ceilings(c))

    weight = jnp.exp(scores[...] - ceil_rep[...]).astype(BF16)
    total = matmul(weight, ones).astype(BF16)
    load_v.wait()
    mixed = lax.dot_general(
        weight.reshape(slots, heads, tokens), v_vm[...], (((2,), (1,)), ((0,), (0,))),
        preferred_element_type=F32,
    ).reshape(tall, dim).astype(BF16)
    both = jnp.concatenate([mixed, total], axis=1)

    def combine(c):
        merged = matmul(held[c], both)
        stat_rows(c, 1, merged[:, dim:])
        acc_out[pl.ds(c * RANK_CHUNK, RANK_CHUNK)] = (
            merged[:, :dim].astype(BF16).reshape(RANK_CHUNK, rows, dim)
        )

    each_chunk(combine)

    each(
        ranks - 1,
        lambda i: send(stat_out.at[rank_at(i)], stat_in.at[rank], 2, (rank_at(i), shard)),
    )
    each(
        ranks - 1,
        lambda i: send(acc_out.at[rank_at(i)], acc_in.at[rank], 3, (rank_at(i), shard)),
    )
    stat_in[rank] = stat_out[rank]
    acc_in[rank] = acc_out[rank]

    drain(stat_in, recv_sem, 2, ranks - 1)
    per_group = LANES // rows
    stats = [
        jnp.sum(stat_in[g : g + per_group], axis=0) for g in range(0, ranks, per_group)
    ]
    ceiling = own_row
    for both in stats:
        ceiling = jnp.maximum(ceiling, both[0:1])
    shift = LANES // 2
    while shift >= rows:
        ceiling = jnp.maximum(ceiling, pltpu.roll(ceiling, shift, 1))
        shift //= 2
    shares = [jnp.exp(both[0:1] - ceiling) for both in stats]
    bottom = sum(share * both[1:2] for share, both in zip(shares, stats))
    shift = LANES // 2
    while shift >= rows:
        bottom = bottom + pltpu.roll(bottom, shift, 1)
        shift //= 2
    own_share = jnp.exp(own_row - ceiling)
    inverse = 1.0 / (bottom + own_share)
    first = iota((rows, LANES), 1) == iota((rows, LANES), 0)
    own_column = jnp.sum(jnp.where(first, own_share * inverse, 0.0), axis=1, keepdims=True)
    result = own_column * per_head(new_v_ref)

    drain(acc_in, recv_sem, 3, ranks - 1)
    for g, share in enumerate(shares):
        factor = jnp.where(row_lane, share * inverse, 0.0)
        high = factor.astype(BF16)
        low = (factor - high.astype(F32)).astype(BF16)
        part = acc_in[g * per_group : (g + 1) * per_group].reshape(LANES, dim)
        result = result + matmul(high, part) + matmul(low, part)
    out_ref[...] = result.astype(BF16)

    drain(meta_all, send_sem, 0, devices - 1)
    drain(q_all, send_sem, 1, ranks - 1)
    drain(stat_out, send_sem, 2, ranks - 1)
    drain(acc_out, send_sem, 3, ranks - 1)


def per_device(
    ranks, shards, queries, new_token_keys, new_token_values, key_pool, value_pool, block_list, context_len
):
    micro, requests, width = queries.shape
    slots, tokens, dim = key_pool.shape
    heads = width // dim
    rows = micro * heads
    rank, shard = lax.axis_index("dp"), lax.axis_index("tp")
    me = rank * shards + shard
    listed = block_list.shape[1]
    position = shard * listed + jnp.arange(listed, dtype=jnp.int32)
    live = jnp.clip(context_len.reshape(micro, 1) - position[None, :] * tokens, 0, tokens)
    pool_row = block_list[:, :, 0] * slots + block_list[:, :, 1]
    entries = micro * listed
    meta = jnp.stack([pool_row.reshape(entries), live.reshape(entries)])
    place = jnp.arange(LANES, dtype=jnp.int32) // entries == lax.rem(me, LANES // entries)
    meta = jnp.where(place[None, :], jnp.tile(meta, (1, LANES // entries)), 0).astype(F32)
    tall = slots * heads
    chunks = ranks // RANK_CHUNK
    chunk_rows = RANK_CHUNK * rows
    vmem = pl.BlockSpec(memory_space=pltpu.VMEM)
    anywhere = pl.BlockSpec(memory_space=pl.ANY)
    out = pl.pallas_call(
        partial(kernel, ranks, shards, micro, heads),
        out_shape=jax.ShapeDtypeStruct((rows, dim), BF16),
        in_specs=[vmem, vmem, vmem, vmem, anywhere, anywhere],
        out_specs=vmem,
        scratch_shapes=[
            pltpu.VMEM((ranks * shards, 2, LANES), F32),
            pltpu.VMEM((ranks, rows, dim), BF16),
            pltpu.VMEM((slots, tokens, dim), BF16),
            pltpu.VMEM((slots, tokens, dim), BF16),
            pltpu.VMEM((chunks, tall, chunk_rows), BF16),
            pltpu.VMEM((chunks, chunk_rows, tall), BF16),
            pltpu.VMEM((tall, dim), F32),
            pltpu.VMEM((tall, tokens), F32),
            pltpu.VMEM((tall, LANES), F32),
            pltpu.VMEM((ranks, rows, dim), BF16),
            pltpu.VMEM((ranks, 2, LANES), F32),
            pltpu.VMEM((ranks, rows, dim), BF16),
            pltpu.VMEM((ranks, 2, LANES), F32),
            pltpu.SemaphoreType.DMA((2,)),
            pltpu.SemaphoreType.DMA((4,)),
            pltpu.SemaphoreType.DMA((4,)),
        ],
        compiler_params=pltpu.CompilerParams(
            collective_id=0, has_side_effects=True, vmem_limit_bytes=56 * 1024 * 1024
        ),
        name="paged_decode",
    )(
        meta,
        queries.reshape(rows, dim),
        new_token_keys.reshape(micro, dim),
        new_token_values.reshape(micro, dim),
        key_pool,
        value_pool,
    )
    return out.reshape(micro, requests, width)


def solution(mesh):
    placed = (
        P(None, "dp", "tp"),
        P(None, "dp", "tp"),
        P(None, "dp", "tp"),
        P("dp", None, "tp"),
        P("dp", None, "tp"),
        P(None, ("dp", "tp"), None),
        P(None, "dp"),
    )
    return jax.shard_map(
        partial(per_device, mesh.shape["dp"], mesh.shape["tp"]),
        mesh=mesh, in_specs=placed, out_specs=P(None, "dp", "tp"), check_vma=False,
    )
```

```python
from functools import partial

import jax
import jax.numpy as jnp
from jax import lax
from jax.experimental import pallas as pl
from jax.experimental.pallas import tpu as pltpu
from jax.sharding import PartitionSpec as P

F32, BF16 = jnp.float32, jnp.bfloat16
LOW = -1e30
LANES = 128
RANK_CHUNK = 8
ROLLED_FROM = 64


def each(count, body):
    if count < ROLLED_FROM:
        for index in range(count):
            body(index)
    else:
        pl.loop(0, count)(body)


def iota(shape, axis):
    return lax.broadcasted_iota(jnp.int32, shape, axis)


def over(values, size):
    if size & (size - 1):
        return values // size
    return lax.shift_right_logical(values, jnp.full_like(values, size.bit_length() - 1))


def within(values, size):
    return values - over(values, size) * size if size & (size - 1) else values & (size - 1)


def matmul(a, b):
    return jnp.dot(a, b, preferred_element_type=F32)


def kernel(
    ranks, shards, micro, heads,
    q_hbm, new_k_hbm, new_v_hbm, list_hbm, length_hbm, k_hbm, v_hbm, out_ref,
    q_vm, new_k_vm, new_v_vm, list_vm, length_vm, meta_all, q_all, k_vm, v_vm, pick, held, q_sel, scores, ceil_rep, acc_out, stat_out,
    acc_in, stat_in, load_sem, send_sem, recv_sem,
):
    devices = ranks * shards
    slots, tokens, dim = k_vm.shape
    rows = micro * heads
    tall = slots * heads
    chunk_rows = RANK_CHUNK * rows
    chunks = ranks // RANK_CHUNK
    scale = dim ** (-0.5)
    rank, shard = lax.axis_index("dp"), lax.axis_index("tp")
    me = rank * shards + shard

    def load(src, dst, which):
        copy = pltpu.make_async_copy(src, dst, load_sem.at[which])
        copy.start()
        return copy

    small = [
        load(list_hbm, list_vm, 2), load(length_hbm, length_vm, 3), load(q_hbm, q_vm, 4),
        load(new_k_hbm, new_k_vm, 5), load(new_v_hbm, new_v_vm, 6),
    ]
    load_k, load_v = load(k_hbm, k_vm, 0), load(v_hbm, v_vm, 1)

    def after(here, step, size):
        moved = here + step
        return jnp.where(moved >= size, moved - size, moved)

    def rank_at(step):
        return after(rank, step + 1, ranks)

    shard_at = [shard] + [after(shard, step, shards) for step in range(1, shards)]

    def everyone(body):
        for other in shard_at[1:]:
            body(rank, other)

        def rank_body(step):
            there = rank_at(step)
            for other in shard_at:
                body(there, other)

        each(ranks - 1, rank_body)

    barrier = pltpu.get_barrier_semaphore()

    def greet(there, other):
        pl.semaphore_signal(
            barrier, inc=1, device_id=(there, other), device_id_type=pl.DeviceIdType.MESH
        )

    everyone(greet)

    lane = iota((1, LANES), 1)
    listed = list_vm.shape[2]
    entries = micro * listed
    per_row = LANES // entries
    offset = within(me, per_row) * entries
    for copy in small:
        copy.wait()
    blank = jnp.zeros((1, LANES - listed), F32)
    slot = within(lane, entries)
    pool_rows = jnp.zeros((1, LANES), F32)
    count = jnp.zeros((1, LANES), jnp.int32)
    for m in range(micro):
        listing = list_vm[m]
        pool = (listing[0:1] * slots + listing[1:2]).astype(F32)
        pool = jnp.concatenate([pool, blank], axis=1)
        pool_rows = pool_rows + (pltpu.roll(pool, m * listed, 1) if m else pool)
        position = shard * listed + slot - m * listed
        left = jnp.clip(length_vm[0:1, m : m + 1] - position * tokens, 0, tokens)
        count = jnp.where(over(slot, listed) == m, left, count)
    width = entries
    while width < LANES:
        pool_rows = pool_rows + pltpu.roll(pool_rows, width, 1)
        width *= 2
    mine = (lane >= offset) & (lane < offset + entries)
    meta_all[me, 0:1] = jnp.where(mine, pool_rows, 0.0)
    meta_all[me, 1:2] = jnp.where(mine, count.astype(F32), 0.0)
    q_wide = q_vm[0].astype(F32)
    own_q = jnp.concatenate(
        [
            q_wide[m : m + 1, n * dim : (n + 1) * dim] for m in range(micro) for n in range(heads)
        ], 0,
    )
    q_all[rank] = own_q.astype(BF16)
    pl.semaphore_wait(barrier, devices - 1)

    def send(src, dst, which, target):
        pltpu.make_async_remote_copy(
            src_ref=src, dst_ref=dst, send_sem=send_sem.at[which], recv_sem=recv_sem.at[which],
            device_id=target, device_id_type=pl.DeviceIdType.MESH,
        ).start()

    def drain(ref, sem, which, count):
        part = ref.at[pl.ds(0, count)]
        pltpu.make_async_copy(part, part, sem.at[which]).wait()

    everyone(lambda there, other: send(meta_all.at[me], meta_all.at[me], 0, (there, other)))
    each(ranks - 1, lambda i: send(q_all.at[rank], q_all.at[rank], 1, (rank_at(i), shard)))

    row_lane = within(iota((rows, LANES), 1), rows) == iota((rows, LANES), 0)
    spread = (over(iota((tall, slots), 0), heads) == iota((tall, slots), 1)).astype(F32).astype(BF16)
    spread_t = over(iota((slots, tall), 1), heads) == iota((slots, tall), 0)
    ones = jnp.ones((LANES, LANES), BF16)

    def per_head(ref):
        flat = ref[0].astype(F32)
        return jnp.concatenate(
            [jnp.broadcast_to(flat[m : m + 1], (heads, dim)) for m in range(micro)], 0
        )

    own = jnp.sum(own_q * per_head(new_k_vm), axis=1, keepdims=True) * scale
    own_row = jnp.sum(jnp.where(row_lane, own, 0.0), axis=0, keepdims=True)

    drain(meta_all, recv_sem, 0, devices - 1)
    slot_row = (rank * slots + iota((slots, LANES), 0)).astype(F32)

    def find(group, carry):
        request, live = carry
        parts = meta_all[pl.ds(group * per_row, per_row)]
        both = jnp.sum(parts, axis=0)
        owner = over(group * per_row + over(lane, entries), shards)
        name = (owner * micro + over(within(lane, entries), listed)).astype(F32)
        match = jnp.broadcast_to(both[0:1], (slots, LANES)) == slot_row
        request = request + jnp.where(match, name, 0.0)
        live = live + jnp.where(match, both[1:2], 0.0)
        return request, live

    found = (jnp.zeros((slots, LANES), F32), jnp.zeros((slots, LANES), F32))
    groups = devices // per_row
    if groups < 16:
        for group in range(groups):
            found = find(group, found)
    else:
        found = lax.fori_loop(0, groups, find, found)
    summed = matmul(jnp.concatenate(found, axis=0).astype(BF16), ones)
    request = summed[:slots]
    wide = matmul(
        spread, jnp.concatenate([request, summed[slots:]], axis=1).astype(BF16)
    )
    request_tall, live_tall = wide[:, :LANES], wide[:, LANES:]
    target = request_tall * heads + within(iota((tall, LANES), 0), heads).astype(F32)
    target_row = jnp.sum(
        jnp.where(spread_t, jnp.concatenate([request] * (tall // LANES), axis=1), 0.0),
        axis=0, keepdims=True,
    ) * heads + within(iota((1, tall), 1), heads).astype(F32)

    def choose(c):
        for at in range(0, chunk_rows, LANES):
            column = (c * chunk_rows + at + iota((tall, LANES), 1)).astype(F32)
            pick[c, :, at : at + LANES] = jnp.where(target == column, 1.0, 0.0).astype(BF16)
        held[c] = jnp.where(
            (c * chunk_rows + iota((chunk_rows, tall), 0)).astype(F32) == target_row, 1.0, 0.0
        ).astype(BF16)

    each_chunk = lambda body: body(0) if chunks == 1 else pl.loop(0, chunks)(body)
    each_chunk(choose)

    drain(q_all, recv_sem, 1, ranks - 1)
    if chunks == 1:
        q_sel[...] = matmul(pick[0], q_all[...].reshape(chunk_rows, dim))
    else:
        q_sel[...] = jnp.zeros((tall, dim), F32)

        @pl.loop(0, chunks)
        def _(c):
            part = q_all[pl.ds(c * RANK_CHUNK, RANK_CHUNK)].reshape(chunk_rows, dim)
            q_sel[...] += matmul(pick[c], part)

    load_k.wait()
    batched = (((2,), (2,)), ((0,), (0,)))
    raw = lax.dot_general(
        q_sel[...].astype(BF16).reshape(slots, heads, dim), k_vm[...], batched,
        preferred_element_type=F32,
    ).reshape(tall, tokens) * scale
    alive = iota((tall, tokens), 1).astype(F32) < live_tall
    raw = jnp.where(alive, raw, LOW)
    scores[...] = raw
    peak = jnp.max(raw, axis=1, keepdims=True)

    def ceilings(c):
        name = (c * RANK_CHUNK * micro + iota((tall, LANES), 1)).astype(F32)
        best = jnp.where(request_tall == name, peak, LOW).reshape(slots, heads, LANES)
        best = jnp.max(best, axis=0).astype(BF16).astype(F32)
        top = jnp.concatenate(
            [
                jnp.broadcast_to(best[:, r : r + 1], (heads, LANES))
                for r in range(RANK_CHUNK * micro)
            ], 0,
        )
        stat_rows(c, 0, top)
        return top.astype(BF16)

    lane_slot = within(rank, LANES // rows) * rows

    def stat_rows(c, which, values):
        mine = iota((rows, LANES), 1) == iota((rows, LANES), 0) + lane_slot
        for o in range(RANK_CHUNK):
            part = jnp.where(mine, values[o * rows : (o + 1) * rows], 0.0)
            stat_out[c * RANK_CHUNK + o, which : which + 1] = jnp.sum(part, axis=0, keepdims=True)

    if chunks == 1:
        ceil_rep[...] = matmul(pick[0], ceilings(0))
    else:
        ceil_rep[...] = jnp.zeros((tall, LANES), F32)

        @pl.loop(0, chunks)
        def _(c):
            ceil_rep[...] += matmul(pick[c], ceilings(c))

    weight = jnp.exp(scores[...] - ceil_rep[...]).astype(BF16)
    total = matmul(weight, ones).astype(BF16)
    load_v.wait()
    mixed = lax.dot_general(
        weight.reshape(slots, heads, tokens), v_vm[...], (((2,), (1,)), ((0,), (0,))),
        preferred_element_type=F32,
    ).reshape(tall, dim).astype(BF16)
    both = jnp.concatenate([mixed, total], axis=1)

    def combine(c):
        merged = matmul(held[c], both)
        stat_rows(c, 1, merged[:, dim:])
        acc_out[pl.ds(c * RANK_CHUNK, RANK_CHUNK)] = (
            merged[:, :dim].astype(BF16).reshape(RANK_CHUNK, rows, dim)
        )

    each_chunk(combine)

    each(
        ranks - 1,
        lambda i: send(stat_out.at[rank_at(i)], stat_in.at[rank], 2, (rank_at(i), shard)),
    )
    each(
        ranks - 1,
        lambda i: send(acc_out.at[rank_at(i)], acc_in.at[rank], 3, (rank_at(i), shard)),
    )
    stat_in[rank] = stat_out[rank]
    acc_in[rank] = acc_out[rank]

    drain(stat_in, recv_sem, 2, ranks - 1)
    per_group = LANES // rows
    stats = [
        jnp.sum(stat_in[g : g + per_group], axis=0) for g in range(0, ranks, per_group)
    ]
    ceiling = own_row
    for both in stats:
        ceiling = jnp.maximum(ceiling, both[0:1])
    shift = LANES // 2
    while shift >= rows:
        ceiling = jnp.maximum(ceiling, pltpu.roll(ceiling, shift, 1))
        shift //= 2
    shares = [jnp.exp(both[0:1] - ceiling) for both in stats]
    bottom = sum(share * both[1:2] for share, both in zip(shares, stats))
    shift = LANES // 2
    while shift >= rows:
        bottom = bottom + pltpu.roll(bottom, shift, 1)
        shift //= 2
    own_share = jnp.exp(own_row - ceiling)
    inverse = 1.0 / (bottom + own_share)
    first = iota((rows, LANES), 1) == iota((rows, LANES), 0)
    own_column = jnp.sum(jnp.where(first, own_share * inverse, 0.0), axis=1, keepdims=True)
    result = own_column * per_head(new_v_vm)

    drain(acc_in, recv_sem, 3, ranks - 1)
    for g, share in enumerate(shares):
        factor = jnp.where(row_lane, share * inverse, 0.0)
        high = factor.astype(BF16)
        low = (factor - high.astype(F32)).astype(BF16)
        part = acc_in[g * per_group : (g + 1) * per_group].reshape(LANES, dim)
        result = result + matmul(high, part) + matmul(low, part)
    for n in range(heads):
        pair = [result[m * heads + n : m * heads + n + 1] for m in range(micro)]
        out_ref[0, :, n * dim : (n + 1) * dim] = jnp.concatenate(pair, axis=0).astype(BF16)

    drain(meta_all, send_sem, 0, devices - 1)
    drain(q_all, send_sem, 1, ranks - 1)
    drain(stat_out, send_sem, 2, ranks - 1)
    drain(acc_out, send_sem, 3, ranks - 1)


def per_device(
    ranks, shards, queries, new_token_keys, new_token_values, key_pool, value_pool, block_list, context_len
):
    micro, requests, width = queries.shape
    slots, tokens, dim = key_pool.shape
    heads = width // dim
    rows = micro * heads
    queries, new_token_keys, new_token_values = (
        x.transpose(1, 0, 2) for x in (queries, new_token_keys, new_token_values)
    )
    block_list, context_len = block_list.transpose(0, 2, 1), context_len.transpose(1, 0)
    tall = slots * heads
    chunks = ranks // RANK_CHUNK
    chunk_rows = RANK_CHUNK * rows
    vmem = pl.BlockSpec(memory_space=pltpu.VMEM)
    anywhere = pl.BlockSpec(memory_space=pl.ANY)
    out = pl.pallas_call(
        partial(kernel, ranks, shards, micro, heads),
        out_shape=jax.ShapeDtypeStruct(queries.shape, BF16),
        in_specs=[anywhere] * 7,
        out_specs=vmem,
        scratch_shapes=[
            pltpu.VMEM(queries.shape, BF16),
            pltpu.VMEM(new_token_keys.shape, BF16),
            pltpu.VMEM(new_token_values.shape, BF16),
            pltpu.VMEM(block_list.shape, jnp.int32),
            pltpu.VMEM(context_len.shape, jnp.int32),
            pltpu.VMEM((ranks * shards, 2, LANES), F32),
            pltpu.VMEM((ranks, rows, dim), BF16),
            pltpu.VMEM((slots, tokens, dim), BF16),
            pltpu.VMEM((slots, tokens, dim), BF16),
            pltpu.VMEM((chunks, tall, chunk_rows), BF16),
            pltpu.VMEM((chunks, chunk_rows, tall), BF16),
            pltpu.VMEM((tall, dim), F32),
            pltpu.VMEM((tall, tokens), F32),
            pltpu.VMEM((tall, LANES), F32),
            pltpu.VMEM((ranks, rows, dim), BF16),
            pltpu.VMEM((ranks, 2, LANES), F32),
            pltpu.VMEM((ranks, rows, dim), BF16),
            pltpu.VMEM((ranks, 2, LANES), F32),
            pltpu.SemaphoreType.DMA((7,)),
            pltpu.SemaphoreType.DMA((4,)),
            pltpu.SemaphoreType.DMA((4,)),
        ],
        compiler_params=pltpu.CompilerParams(
            collective_id=0, has_side_effects=True, vmem_limit_bytes=56 * 1024 * 1024
        ),
        name="paged_decode",
    )(
        queries, new_token_keys, new_token_values, block_list, context_len, key_pool, value_pool
    )
    return out.transpose(1, 0, 2)


def solution(mesh):
    placed = (
        P(None, "dp", "tp"),
        P(None, "dp", "tp"),
        P(None, "dp", "tp"),
        P("dp", None, "tp"),
        P("dp", None, "tp"),
        P(None, ("dp", "tp"), None),
        P(None, "dp"),
    )
    return jax.shard_map(
        partial(per_device, mesh.shape["dp"], mesh.shape["tp"]),
        mesh=mesh, in_specs=placed, out_specs=P(None, "dp", "tp"), check_vma=False,
    )
```

```python
from functools import partial

import jax
import jax.numpy as jnp
from jax import lax
from jax.experimental import pallas as pl
from jax.experimental.pallas import tpu as pltpu
from jax.sharding import PartitionSpec as P

F32, BF16 = jnp.float32, jnp.bfloat16
LOW = -1e30
LANES = 128
RANK_CHUNK = 8
VMEM_BYTES = 52 << 20
ROLLED_FROM = 64


def each(count, body):
    if count < ROLLED_FROM:
        for index in range(count):
            body(index)
    else:
        pl.loop(0, count)(body)


def iota(shape, axis):
    return lax.broadcasted_iota(jnp.int32, shape, axis)


def over(values, size):
    if size & (size - 1):
        return values // size
    return lax.shift_right_logical(values, jnp.full_like(values, size.bit_length() - 1))


def within(values, size):
    return values - over(values, size) * size if size & (size - 1) else values & (size - 1)


def matmul(a, b):
    return jnp.dot(a, b, preferred_element_type=F32)


def kernel(
    ranks, shards, micro, heads,
    q_hbm, new_k_hbm, new_v_hbm, list_hbm, length_hbm, k_hbm, v_hbm, out_ref,
    q_vm, new_k_vm, new_v_vm, list_vm, length_vm, meta_all, q_all, k_vm, v_vm, pick, held, q_sel, ceil_rep, acc_out, stat_out,
    acc_in, stat_in, load_sem, send_sem, recv_sem,
):
    devices = ranks * shards
    slots, tokens, dim = k_vm.shape
    rows = micro * heads
    tall = slots * heads
    chunk_rows = RANK_CHUNK * rows
    chunks = ranks // RANK_CHUNK
    scale = dim ** (-0.5)
    rank, shard = lax.axis_index("dp"), lax.axis_index("tp")
    me = rank * shards + shard

    def load(src, dst, which):
        copy = pltpu.make_async_copy(src, dst, load_sem.at[which])
        copy.start()
        return copy

    small = [
        load(list_hbm, list_vm, 2), load(length_hbm, length_vm, 3), load(q_hbm, q_vm, 4),
        load(new_k_hbm, new_k_vm, 5), load(new_v_hbm, new_v_vm, 6),
    ]
    load_k, load_v = load(k_hbm, k_vm, 0), load(v_hbm, v_vm, 1)

    def after(here, step, size):
        moved = here + step
        return jnp.where(moved >= size, moved - size, moved)

    def rank_at(step):
        return after(rank, step + 1, ranks)

    shard_at = [shard] + [after(shard, step, shards) for step in range(1, shards)]

    def everyone(body):
        for other in shard_at[1:]:
            body(rank, other)

        def rank_body(step):
            there = rank_at(step)
            for other in shard_at:
                body(there, other)

        each(ranks - 1, rank_body)

    barrier = pltpu.get_barrier_semaphore()

    def greet(there, other):
        pl.semaphore_signal(
            barrier, inc=1, device_id=(there, other), device_id_type=pl.DeviceIdType.MESH
        )

    everyone(greet)

    lane = iota((1, LANES), 1)
    listed = list_vm.shape[2]
    entries = micro * listed
    per_row = LANES // entries
    offset = within(me, per_row) * entries
    for copy in small:
        copy.wait()
    blank = jnp.zeros((1, LANES - listed), F32)
    slot = within(lane, entries)
    pool_rows = jnp.zeros((1, LANES), F32)
    count = jnp.zeros((1, LANES), jnp.int32)
    for m in range(micro):
        listing = list_vm[m]
        pool = (listing[0:1] * slots + listing[1:2]).astype(F32)
        pool = jnp.concatenate([pool, blank], axis=1)
        pool_rows = pool_rows + (pltpu.roll(pool, m * listed, 1) if m else pool)
        position = shard * listed + slot - m * listed
        left = jnp.clip(length_vm[0:1, m : m + 1] - position * tokens, 0, tokens)
        count = jnp.where(over(slot, listed) == m, left, count)
    width = entries
    while width < LANES:
        pool_rows = pool_rows + pltpu.roll(pool_rows, width, 1)
        width *= 2
    mine = (lane >= offset) & (lane < offset + entries)
    meta_all[me, 0:1] = jnp.where(mine, pool_rows, 0.0)
    meta_all[me, 1:2] = jnp.where(mine, count.astype(F32), 0.0)
    q_wide = q_vm[0].astype(F32)
    own_q = jnp.concatenate(
        [
            q_wide[m : m + 1, n * dim : (n + 1) * dim] for m in range(micro) for n in range(heads)
        ], 0,
    )
    q_all[rank] = own_q.astype(BF16)
    pl.semaphore_wait(barrier, devices - 1)

    def send(src, dst, which, target):
        pltpu.make_async_remote_copy(
            src_ref=src, dst_ref=dst, send_sem=send_sem.at[which], recv_sem=recv_sem.at[which],
            device_id=target, device_id_type=pl.DeviceIdType.MESH,
        ).start()

    def drain(ref, sem, which, count):
        part = ref.at[pl.ds(0, count)]
        pltpu.make_async_copy(part, part, sem.at[which]).wait()

    everyone(lambda there, other: send(meta_all.at[me], meta_all.at[me], 0, (there, other)))
    each(ranks - 1, lambda i: send(q_all.at[rank], q_all.at[rank], 1, (rank_at(i), shard)))

    row_lane = within(iota((rows, LANES), 1), rows) == iota((rows, LANES), 0)
    spread_t = over(iota((slots, tall), 1), heads) == iota((slots, tall), 0)
    ones = jnp.ones((LANES, LANES), BF16)

    def per_head(ref):
        flat = ref[0].astype(F32)
        return jnp.concatenate(
            [jnp.broadcast_to(flat[m : m + 1], (heads, dim)) for m in range(micro)], 0
        )

    own = jnp.sum(own_q * per_head(new_k_vm), axis=1, keepdims=True) * scale
    own_row = jnp.sum(jnp.where(row_lane, own, 0.0), axis=0, keepdims=True)

    drain(meta_all, recv_sem, 0, devices - 1)
    slot_row = (rank * slots + iota((slots, LANES), 0)).astype(F32)

    def find(group, carry):
        request, live = carry
        parts = meta_all[pl.ds(group * per_row, per_row)]
        both = jnp.sum(parts, axis=0)
        owner = over(group * per_row + over(lane, entries), shards)
        name = (owner * micro + over(within(lane, entries), listed)).astype(F32)
        match = jnp.broadcast_to(both[0:1], (slots, LANES)) == slot_row
        request = request + jnp.where(match, name, 0.0)
        live = live + jnp.where(match, both[1:2], 0.0)
        return request, live

    found = (jnp.zeros((slots, LANES), F32), jnp.zeros((slots, LANES), F32))
    groups = devices // per_row
    if groups < 16:
        for group in range(groups):
            found = find(group, found)
    else:
        found = lax.fori_loop(0, groups, find, found)
    summed = matmul(jnp.concatenate(found, axis=0).astype(BF16), ones)
    request = summed[:slots]
    def heads_of(values):
        return jnp.concatenate(
            [jnp.broadcast_to(values[i : i + 1], (heads, LANES)) for i in range(slots)], 0
        )

    request_tall, live_tall = heads_of(request), heads_of(summed[slots:])
    target = request_tall * heads + within(iota((tall, LANES), 0), heads).astype(F32)
    target_row = jnp.sum(
        jnp.where(spread_t, jnp.concatenate([request] * (tall // LANES), axis=1), 0.0),
        axis=0, keepdims=True,
    ) * heads + within(iota((1, tall), 1), heads).astype(F32)

    def choose(c):
        for at in range(0, chunk_rows, LANES):
            column = (c * chunk_rows + at + iota((tall, LANES), 1)).astype(F32)
            pick[c, :, at : at + LANES] = jnp.where(target == column, 1.0, 0.0).astype(BF16)
        held[c] = jnp.where(
            (c * chunk_rows + iota((chunk_rows, tall), 0)).astype(F32) == target_row, 1.0, 0.0
        ).astype(BF16)

    each_chunk = lambda body: body(0) if chunks == 1 else pl.loop(0, chunks)(body)
    each_chunk(choose)

    drain(q_all, recv_sem, 1, ranks - 1)
    if chunks == 1:
        q_sel[...] = matmul(pick[0], q_all[...].reshape(chunk_rows, dim))
    else:
        q_sel[...] = jnp.zeros((tall, dim), F32)

        @pl.loop(0, chunks)
        def _(c):
            part = q_all[pl.ds(c * RANK_CHUNK, RANK_CHUNK)].reshape(chunk_rows, dim)
            q_sel[...] += matmul(pick[c], part)

    load_k.wait()
    batched = (((2,), (2,)), ((0,), (0,)))
    raw = lax.dot_general(
        q_sel[...].astype(BF16).reshape(slots, heads, dim), k_vm[...], batched,
        preferred_element_type=F32,
    ).reshape(tall, tokens) * scale
    alive = iota((tall, tokens), 1).astype(F32) < live_tall
    raw = jnp.where(alive, raw, LOW)
    peak = jnp.max(raw, axis=1, keepdims=True)
    weight = jnp.exp(raw - peak).astype(BF16)
    total = matmul(weight, ones)
    load_v.wait()
    mixed = lax.dot_general(
        weight.reshape(slots, heads, tokens), v_vm[...], (((2,), (1,)), ((0,), (0,))),
        preferred_element_type=F32,
    ).reshape(tall, dim)

    def ceilings(c):
        name = (c * RANK_CHUNK * micro + iota((tall, LANES), 1)).astype(F32)
        best = jnp.where(request_tall == name, peak, LOW).reshape(slots, heads, LANES)
        best = jnp.max(best, axis=0).astype(BF16).astype(F32)
        top = jnp.concatenate(
            [
                jnp.broadcast_to(best[:, r : r + 1], (heads, LANES))
                for r in range(RANK_CHUNK * micro)
            ], 0,
        )
        stat_rows(c, 0, top)
        return top.astype(BF16)

    lane_slot = within(rank, LANES // rows) * rows

    def stat_rows(c, which, values):
        mine = iota((rows, LANES), 1) == iota((rows, LANES), 0) + lane_slot
        for o in range(RANK_CHUNK):
            part = jnp.where(mine, values[o * rows : (o + 1) * rows], 0.0)
            stat_out[c * RANK_CHUNK + o, which : which + 1] = jnp.sum(part, axis=0, keepdims=True)

    if chunks == 1:
        ceil_rep[...] = matmul(pick[0], ceilings(0))
    else:
        ceil_rep[...] = jnp.zeros((tall, LANES), F32)

        @pl.loop(0, chunks)
        def _(c):
            ceil_rep[...] += matmul(pick[c], ceilings(c))

    rescale = jnp.exp(peak - ceil_rep[...])
    both = jnp.concatenate([(mixed * rescale).astype(BF16), (total * rescale).astype(BF16)], axis=1)

    def combine(c):
        merged = matmul(held[c], both)
        stat_rows(c, 1, merged[:, dim:])
        acc_out[pl.ds(c * RANK_CHUNK, RANK_CHUNK)] = (
            merged[:, :dim].astype(BF16).reshape(RANK_CHUNK, rows, dim)
        )

    each_chunk(combine)

    each(
        ranks - 1,
        lambda i: send(stat_out.at[rank_at(i)], stat_in.at[rank], 2, (rank_at(i), shard)),
    )
    each(
        ranks - 1,
        lambda i: send(acc_out.at[rank_at(i)], acc_in.at[rank], 3, (rank_at(i), shard)),
    )
    stat_in[rank] = stat_out[rank]
    acc_in[rank] = acc_out[rank]

    drain(stat_in, recv_sem, 2, ranks - 1)
    per_group = LANES // rows
    stats = [
        jnp.sum(stat_in[g : g + per_group], axis=0) for g in range(0, ranks, per_group)
    ]
    ceiling = own_row
    for both in stats:
        ceiling = jnp.maximum(ceiling, both[0:1])
    shift = LANES // 2
    while shift >= rows:
        ceiling = jnp.maximum(ceiling, pltpu.roll(ceiling, shift, 1))
        shift //= 2
    shares = [jnp.exp(both[0:1] - ceiling) for both in stats]
    bottom = sum(share * both[1:2] for share, both in zip(shares, stats))
    shift = LANES // 2
    while shift >= rows:
        bottom = bottom + pltpu.roll(bottom, shift, 1)
        shift //= 2
    own_share = jnp.exp(own_row - ceiling)
    inverse = 1.0 / (bottom + own_share)
    first = iota((rows, LANES), 1) == iota((rows, LANES), 0)
    own_column = jnp.sum(jnp.where(first, own_share * inverse, 0.0), axis=1, keepdims=True)
    result = own_column * per_head(new_v_vm)

    drain(acc_in, recv_sem, 3, ranks - 1)
    for g, share in enumerate(shares):
        factor = jnp.where(row_lane, share * inverse, 0.0)
        high = factor.astype(BF16)
        low = (factor - high.astype(F32)).astype(BF16)
        part = acc_in[g * per_group : (g + 1) * per_group].reshape(LANES, dim)
        result = result + matmul(high, part) + matmul(low, part)
    for n in range(heads):
        pair = [result[m * heads + n : m * heads + n + 1] for m in range(micro)]
        out_ref[0, :, n * dim : (n + 1) * dim] = jnp.concatenate(pair, axis=0).astype(BF16)

    drain(meta_all, send_sem, 0, devices - 1)
    drain(q_all, send_sem, 1, ranks - 1)
    drain(stat_out, send_sem, 2, ranks - 1)
    drain(acc_out, send_sem, 3, ranks - 1)


def per_device(
    ranks, shards, queries, new_token_keys, new_token_values, key_pool, value_pool, block_list, context_len
):
    micro, requests, width = queries.shape
    slots, tokens, dim = key_pool.shape
    heads = width // dim
    rows = micro * heads
    queries, new_token_keys, new_token_values = (
        x.transpose(1, 0, 2) for x in (queries, new_token_keys, new_token_values)
    )
    block_list, context_len = block_list.transpose(0, 2, 1), context_len.transpose(1, 0)
    tall = slots * heads
    chunks = ranks // RANK_CHUNK
    chunk_rows = RANK_CHUNK * rows
    vmem = pl.BlockSpec(memory_space=pltpu.VMEM)
    anywhere = pl.BlockSpec(memory_space=pl.ANY)
    out = pl.pallas_call(
        partial(kernel, ranks, shards, micro, heads),
        out_shape=jax.ShapeDtypeStruct(queries.shape, BF16),
        in_specs=[anywhere] * 7,
        out_specs=vmem,
        scratch_shapes=[
            pltpu.VMEM(queries.shape, BF16),
            pltpu.VMEM(new_token_keys.shape, BF16),
            pltpu.VMEM(new_token_values.shape, BF16),
            pltpu.VMEM(block_list.shape, jnp.int32),
            pltpu.VMEM(context_len.shape, jnp.int32),
            pltpu.VMEM((ranks * shards, 2, LANES), F32),
            pltpu.VMEM((ranks, rows, dim), BF16),
            pltpu.VMEM((slots, tokens, dim), BF16),
            pltpu.VMEM((slots, tokens, dim), BF16),
            pltpu.VMEM((chunks, tall, chunk_rows), BF16),
            pltpu.VMEM((chunks, chunk_rows, tall), BF16),
            pltpu.VMEM((tall, dim), F32),
            pltpu.VMEM((tall, LANES), F32),
            pltpu.VMEM((ranks, rows, dim), BF16),
            pltpu.VMEM((ranks, 2, LANES), F32),
            pltpu.VMEM((ranks, rows, dim), BF16),
            pltpu.VMEM((ranks, 2, LANES), F32),
            pltpu.SemaphoreType.DMA((7,)),
            pltpu.SemaphoreType.DMA((4,)),
            pltpu.SemaphoreType.DMA((4,)),
        ],
        compiler_params=pltpu.CompilerParams(
            collective_id=0, has_side_effects=True, vmem_limit_bytes=VMEM_BYTES
        ),
        name="paged_decode",
    )(
        queries, new_token_keys, new_token_values, block_list, context_len, key_pool, value_pool
    )
    return out.transpose(1, 0, 2)


def solution(mesh):
    placed = (
        P(None, "dp", "tp"),
        P(None, "dp", "tp"),
        P(None, "dp", "tp"),
        P("dp", None, "tp"),
        P("dp", None, "tp"),
        P(None, ("dp", "tp"), None),
        P(None, "dp"),
    )
    return jax.shard_map(
        partial(per_device, mesh.shape["dp"], mesh.shape["tp"]),
        mesh=mesh, in_specs=placed, out_specs=P(None, "dp", "tp"), check_vma=False,
    )
```

```python
from functools import partial

import jax
import jax.numpy as jnp
from jax import lax
from jax.experimental import pallas as pl
from jax.experimental.pallas import tpu as pltpu
from jax.sharding import PartitionSpec as P

F32, BF16 = jnp.float32, jnp.bfloat16
LOW = -1e30
LANES = 128
RANK_CHUNK = 8
VMEM_BYTES = 56 << 20
ROLLED_FROM = 64


def each(count, body):
    if count < ROLLED_FROM:
        for index in range(count):
            body(index)
    else:
        pl.loop(0, count)(body)


def iota(shape, axis):
    return lax.broadcasted_iota(jnp.int32, shape, axis)


def over(values, size):
    if size & (size - 1):
        return values // size
    return lax.shift_right_logical(values, jnp.full_like(values, size.bit_length() - 1))


def within(values, size):
    return values - over(values, size) * size if size & (size - 1) else values & (size - 1)


def matmul(a, b):
    return jnp.dot(a, b, preferred_element_type=F32)


def kernel(
    ranks, shards, micro, heads,
    q_hbm, new_k_hbm, new_v_hbm, list_hbm, length_hbm, k_hbm, v_hbm, out_ref,
    q_vm, new_k_vm, new_v_vm, list_vm, length_vm, meta_own, meta_all, q_all, k_vm, v_vm, pick, held, q_sel, ceil_rep, acc_out, stat_out,
    acc_in, stat_in, load_sem, send_sem, recv_sem,
):
    slots, tokens, dim = k_vm.shape
    rows = micro * heads
    tall = slots * heads
    chunk_rows = RANK_CHUNK * rows
    chunks = ranks // RANK_CHUNK
    scale = dim ** (-0.5)
    rank, shard = lax.axis_index("dp"), lax.axis_index("tp")
    me = rank * shards + shard

    def load(src, dst, which):
        copy = pltpu.make_async_copy(src, dst, load_sem.at[which])
        copy.start()
        return copy

    small = [
        load(list_hbm, list_vm, 2), load(length_hbm, length_vm, 3), load(q_hbm, q_vm, 4),
        load(new_k_hbm, new_k_vm, 5), load(new_v_hbm, new_v_vm, 6),
    ]
    load_k, load_v = load(k_hbm, k_vm, 0), load(v_hbm, v_vm, 1)

    def after(here, step, size):
        moved = here + step
        return jnp.where(moved >= size, moved - size, moved)

    def rank_at(step):
        return after(rank, step + 1, ranks)

    shard_at = [shard] + [after(shard, step, shards) for step in range(1, shards)]

    def peers(body):
        for other in shard_at[1:]:
            body(rank, other)

    def holders(body):
        each(ranks - 1, lambda step: body(rank_at(step)))

    barrier = pltpu.get_barrier_semaphore()

    def greet(there, other):
        pl.semaphore_signal(
            barrier, inc=1, device_id=(there, other), device_id_type=pl.DeviceIdType.MESH
        )

    holders(lambda there: greet(there, shard))
    peers(greet)

    lane = iota((1, LANES), 1)
    listed = list_vm.shape[2]
    entries = micro * listed
    per_row = LANES // entries
    offset = within(me, per_row) * entries
    for copy in small:
        copy.wait()
    blank = jnp.zeros((1, LANES - listed), F32)
    slot = within(lane, entries)
    pool_rows = jnp.zeros((1, LANES), F32)
    count = jnp.zeros((1, LANES), jnp.int32)
    for m in range(micro):
        listing = list_vm[m]
        pool = (listing[0:1] * slots + listing[1:2]).astype(F32)
        pool = jnp.concatenate([pool, blank], axis=1)
        pool_rows = pool_rows + (pltpu.roll(pool, m * listed, 1) if m else pool)
        position = shard * listed + slot - m * listed
        left = jnp.clip(length_vm[0:1, m : m + 1] - position * tokens, 0, tokens)
        count = jnp.where(over(slot, listed) == m, left, count)
    width = entries
    while width < LANES:
        pool_rows = pool_rows + pltpu.roll(pool_rows, width, 1)
        width *= 2
    mine = (lane >= offset) & (lane < offset + entries)
    meta_own[shard, 0:1] = jnp.where(mine, pool_rows, 0.0)
    meta_own[shard, 1:2] = jnp.where(mine, count.astype(F32), 0.0)
    q_wide = q_vm[0].astype(F32)
    own_q = jnp.concatenate(
        [
            q_wide[m : m + 1, n * dim : (n + 1) * dim] for m in range(micro) for n in range(heads)
        ], 0,
    )
    q_all[rank] = own_q.astype(BF16)
    pl.semaphore_wait(barrier, ranks - 1 + shards - 1)

    def send(src, dst, which, target):
        pltpu.make_async_remote_copy(
            src_ref=src, dst_ref=dst, send_sem=send_sem.at[which], recv_sem=recv_sem.at[which],
            device_id=target, device_id_type=pl.DeviceIdType.MESH,
        ).start()

    def drain(ref, sem, which, count):
        part = ref.at[pl.ds(0, count)]
        pltpu.make_async_copy(part, part, sem.at[which]).wait()

    peers(lambda there, other: send(meta_own.at[shard], meta_own.at[shard], 4, (there, other)))
    holders(lambda there: send(q_all.at[rank], q_all.at[rank], 1, (there, shard)))
    drain(meta_own, recv_sem, 4, shards - 1)
    meta_all[rank] = jnp.sum(meta_own[...], axis=0)
    holders(lambda there: send(meta_all.at[rank], meta_all.at[rank], 0, (there, shard)))

    row_lane = within(iota((rows, LANES), 1), rows) == iota((rows, LANES), 0)
    spread_t = over(iota((slots, tall), 1), heads) == iota((slots, tall), 0)
    ones = jnp.ones((LANES, LANES), BF16)

    def per_head(ref):
        flat = ref[0].astype(F32)
        return jnp.concatenate(
            [jnp.broadcast_to(flat[m : m + 1], (heads, dim)) for m in range(micro)], 0
        )

    own = jnp.sum(own_q * per_head(new_k_vm), axis=1, keepdims=True) * scale
    own_row = jnp.sum(jnp.where(row_lane, own, 0.0), axis=0, keepdims=True)

    drain(meta_all, recv_sem, 0, ranks - 1)
    slot_row = (rank * slots + iota((slots, LANES), 0)).astype(F32)

    def find(group, carry):
        request, live = carry
        parts = meta_all[pl.ds(group * share, share)]
        both = jnp.sum(parts, axis=0)
        owner = over(group * per_row + over(lane, entries), shards)
        name = (owner * micro + over(within(lane, entries), listed)).astype(F32)
        match = jnp.broadcast_to(both[0:1], (slots, LANES)) == slot_row
        request = request + jnp.where(match, name, 0.0)
        live = live + jnp.where(match, both[1:2], 0.0)
        return request, live

    found = (jnp.zeros((slots, LANES), F32), jnp.zeros((slots, LANES), F32))
    share = per_row // shards
    groups = ranks // share
    if groups < 16:
        for group in range(groups):
            found = find(group, found)
    else:
        found = lax.fori_loop(0, groups, find, found)
    summed = matmul(jnp.concatenate(found, axis=0).astype(BF16), ones)
    request = summed[:slots]
    def heads_of(values):
        return jnp.concatenate(
            [jnp.broadcast_to(values[i : i + 1], (heads, LANES)) for i in range(slots)], 0
        )

    request_tall, live_tall = heads_of(request), heads_of(summed[slots:])
    target = request_tall * heads + within(iota((tall, LANES), 0), heads).astype(F32)
    target_row = jnp.sum(
        jnp.where(spread_t, jnp.concatenate([request] * (tall // LANES), axis=1), 0.0),
        axis=0, keepdims=True,
    ) * heads + within(iota((1, tall), 1), heads).astype(F32)

    def choose(c):
        for at in range(0, chunk_rows, LANES):
            column = (c * chunk_rows + at + iota((tall, LANES), 1)).astype(F32)
            pick[c, :, at : at + LANES] = jnp.where(target == column, 1.0, 0.0).astype(BF16)
        held[c] = jnp.where(
            (c * chunk_rows + iota((chunk_rows, tall), 0)).astype(F32) == target_row, 1.0, 0.0
        ).astype(BF16)

    each_chunk = lambda body: body(0) if chunks == 1 else pl.loop(0, chunks)(body)
    each_chunk(choose)

    drain(q_all, recv_sem, 1, ranks - 1)
    if chunks == 1:
        q_sel[...] = matmul(pick[0], q_all[...].reshape(chunk_rows, dim))
    else:
        q_sel[...] = jnp.zeros((tall, dim), F32)

        @pl.loop(0, chunks)
        def _(c):
            part = q_all[pl.ds(c * RANK_CHUNK, RANK_CHUNK)].reshape(chunk_rows, dim)
            q_sel[...] += matmul(pick[c], part)

    load_k.wait()
    batched = (((2,), (2,)), ((0,), (0,)))
    raw = lax.dot_general(
        q_sel[...].astype(BF16).reshape(slots, heads, dim), k_vm[...], batched,
        preferred_element_type=F32,
    ).reshape(tall, tokens) * scale
    alive = iota((tall, tokens), 1).astype(F32) < live_tall
    raw = jnp.where(alive, raw, LOW)
    peak = jnp.max(raw, axis=1, keepdims=True)
    weight = jnp.exp(raw - peak).astype(BF16)
    total = matmul(weight, ones)
    load_v.wait()
    mixed = lax.dot_general(
        weight.reshape(slots, heads, tokens), v_vm[...], (((2,), (1,)), ((0,), (0,))),
        preferred_element_type=F32,
    ).reshape(tall, dim)

    def ceilings(c):
        name = (c * RANK_CHUNK * micro + iota((tall, LANES), 1)).astype(F32)
        best = jnp.where(request_tall == name, peak, LOW).reshape(slots, heads, LANES)
        best = jnp.max(best, axis=0).astype(BF16).astype(F32)
        top = jnp.concatenate(
            [
                jnp.broadcast_to(best[:, r : r + 1], (heads, LANES))
                for r in range(RANK_CHUNK * micro)
            ], 0,
        )
        stat_rows(c, 0, top)
        return top.astype(BF16)

    lane_slot = within(rank, LANES // rows) * rows

    def stat_rows(c, which, values):
        mine = iota((rows, LANES), 1) == iota((rows, LANES), 0) + lane_slot
        for o in range(RANK_CHUNK):
            part = jnp.where(mine, values[o * rows : (o + 1) * rows], 0.0)
            stat_out[c * RANK_CHUNK + o, which : which + 1] = jnp.sum(part, axis=0, keepdims=True)

    if chunks == 1:
        ceil_rep[...] = matmul(pick[0], ceilings(0))
    else:
        ceil_rep[...] = jnp.zeros((tall, LANES), F32)

        @pl.loop(0, chunks)
        def _(c):
            ceil_rep[...] += matmul(pick[c], ceilings(c))

    rescale = jnp.exp(peak - ceil_rep[...])
    both = jnp.concatenate([(mixed * rescale).astype(BF16), (total * rescale).astype(BF16)], axis=1)

    def combine(c):
        merged = matmul(held[c], both)
        stat_rows(c, 1, merged[:, dim:])
        acc_out[pl.ds(c * RANK_CHUNK, RANK_CHUNK)] = (
            merged[:, :dim].astype(BF16).reshape(RANK_CHUNK, rows, dim)
        )

    each_chunk(combine)

    holders(lambda there: send(stat_out.at[there], stat_in.at[rank], 2, (there, shard)))
    holders(lambda there: send(acc_out.at[there], acc_in.at[rank], 3, (there, shard)))
    stat_in[rank] = stat_out[rank]
    acc_in[rank] = acc_out[rank]

    drain(stat_in, recv_sem, 2, ranks - 1)
    per_group = LANES // rows
    stats = [
        jnp.sum(stat_in[g : g + per_group], axis=0) for g in range(0, ranks, per_group)
    ]
    ceiling = own_row
    for both in stats:
        ceiling = jnp.maximum(ceiling, both[0:1])
    shift = LANES // 2
    while shift >= rows:
        ceiling = jnp.maximum(ceiling, pltpu.roll(ceiling, shift, 1))
        shift //= 2
    shares = [jnp.exp(both[0:1] - ceiling) for both in stats]
    bottom = sum(share * both[1:2] for share, both in zip(shares, stats))
    shift = LANES // 2
    while shift >= rows:
        bottom = bottom + pltpu.roll(bottom, shift, 1)
        shift //= 2
    own_share = jnp.exp(own_row - ceiling)
    inverse = 1.0 / (bottom + own_share)
    first = iota((rows, LANES), 1) == iota((rows, LANES), 0)
    own_column = jnp.sum(jnp.where(first, own_share * inverse, 0.0), axis=1, keepdims=True)
    result = own_column * per_head(new_v_vm)

    drain(acc_in, recv_sem, 3, ranks - 1)
    for g, share in enumerate(shares):
        factor = jnp.where(row_lane, share * inverse, 0.0)
        high = factor.astype(BF16)
        low = (factor - high.astype(F32)).astype(BF16)
        part = acc_in[g * per_group : (g + 1) * per_group].reshape(LANES, dim)
        result = result + matmul(high, part) + matmul(low, part)
    for n in range(heads):
        pair = [result[m * heads + n : m * heads + n + 1] for m in range(micro)]
        out_ref[0, :, n * dim : (n + 1) * dim] = jnp.concatenate(pair, axis=0).astype(BF16)

    drain(meta_own, send_sem, 4, shards - 1)
    drain(meta_all, send_sem, 0, ranks - 1)
    drain(q_all, send_sem, 1, ranks - 1)
    drain(stat_out, send_sem, 2, ranks - 1)
    drain(acc_out, send_sem, 3, ranks - 1)


def per_device(
    ranks, shards, queries, new_token_keys, new_token_values, key_pool, value_pool, block_list, context_len
):
    micro, requests, width = queries.shape
    slots, tokens, dim = key_pool.shape
    heads = width // dim
    rows = micro * heads
    queries, new_token_keys, new_token_values = (
        x.transpose(1, 0, 2) for x in (queries, new_token_keys, new_token_values)
    )
    block_list, context_len = block_list.transpose(0, 2, 1), context_len.transpose(1, 0)
    tall = slots * heads
    chunks = ranks // RANK_CHUNK
    chunk_rows = RANK_CHUNK * rows
    vmem = pl.BlockSpec(memory_space=pltpu.VMEM)
    anywhere = pl.BlockSpec(memory_space=pl.ANY)
    out = pl.pallas_call(
        partial(kernel, ranks, shards, micro, heads),
        out_shape=pltpu.VMEM(queries.shape, BF16),
        in_specs=[anywhere] * 7,
        out_specs=vmem,
        scratch_shapes=[
            pltpu.VMEM(queries.shape, BF16),
            pltpu.VMEM(new_token_keys.shape, BF16),
            pltpu.VMEM(new_token_values.shape, BF16),
            pltpu.VMEM(block_list.shape, jnp.int32),
            pltpu.VMEM(context_len.shape, jnp.int32),
            pltpu.VMEM((shards, 2, LANES), F32),
            pltpu.VMEM((ranks, 2, LANES), F32),
            pltpu.VMEM((ranks, rows, dim), BF16),
            pltpu.VMEM((slots, tokens, dim), BF16),
            pltpu.VMEM((slots, tokens, dim), BF16),
            pltpu.VMEM((chunks, tall, chunk_rows), BF16),
            pltpu.VMEM((chunks, chunk_rows, tall), BF16),
            pltpu.VMEM((tall, dim), F32),
            pltpu.VMEM((tall, LANES), F32),
            pltpu.VMEM((ranks, rows, dim), BF16),
            pltpu.VMEM((ranks, 2, LANES), F32),
            pltpu.VMEM((ranks, rows, dim), BF16),
            pltpu.VMEM((ranks, 2, LANES), F32),
            pltpu.SemaphoreType.DMA((7,)),
            pltpu.SemaphoreType.DMA((5,)),
            pltpu.SemaphoreType.DMA((5,)),
        ],
        compiler_params=pltpu.CompilerParams(
            collective_id=0, has_side_effects=True, vmem_limit_bytes=VMEM_BYTES
        ),
        name="paged_decode",
    )(
        queries, new_token_keys, new_token_values, block_list, context_len, key_pool, value_pool
    )
    return out.transpose(1, 0, 2)


def solution(mesh):
    placed = (
        P(None, "dp", "tp"),
        P(None, "dp", "tp"),
        P(None, "dp", "tp"),
        P("dp", None, "tp"),
        P("dp", None, "tp"),
        P(None, ("dp", "tp"), None),
        P(None, "dp"),
    )
    return jax.shard_map(
        partial(per_device, mesh.shape["dp"], mesh.shape["tp"]),
        mesh=mesh, in_specs=placed, out_specs=P(None, "dp", "tp"), check_vma=False,
    )
```

```python
from functools import partial

import jax
import jax.numpy as jnp
from jax import lax
from jax.experimental import pallas as pl
from jax.experimental.pallas import tpu as pltpu
from jax.sharding import PartitionSpec as P

F32, BF16 = jnp.float32, jnp.bfloat16
LOW = -1e30
LANES = 128
RANK_CHUNK = 8
VMEM_BYTES = 56 << 20
ROLLED_FROM = 64


def each(count, body):
    if count < ROLLED_FROM:
        for index in range(count):
            body(index)
    else:
        pl.loop(0, count)(body)


def iota(shape, axis):
    return lax.broadcasted_iota(jnp.int32, shape, axis)


def over(values, size):
    if size & (size - 1):
        return values // size
    return lax.shift_right_logical(values, jnp.full_like(values, size.bit_length() - 1))


def within(values, size):
    return values - over(values, size) * size if size & (size - 1) else values & (size - 1)


def matmul(a, b):
    return jnp.dot(a, b, preferred_element_type=F32)


def kernel(
    ranks, shards, micro, heads,
    q_hbm, new_k_hbm, new_v_hbm, list_hbm, length_hbm, k_hbm, v_hbm, out_ref,
    q_vm, new_k_vm, new_v_vm, list_vm, length_vm, meta_all, q_all, k_vm, v_vm, pick, held, q_sel, ceil_rep, acc_out, stat_out,
    acc_in, stat_in, load_sem, send_sem, recv_sem,
):
    devices = ranks * shards
    slots, tokens, dim = k_vm.shape
    rows = micro * heads
    tall = slots * heads
    chunk_rows = RANK_CHUNK * rows
    chunks = ranks // RANK_CHUNK
    scale = dim ** (-0.5)
    rank, shard = lax.axis_index("dp"), lax.axis_index("tp")
    me = rank * shards + shard

    def load(src, dst, which):
        copy = pltpu.make_async_copy(src, dst, load_sem.at[which])
        copy.start()
        return copy

    small = [
        load(list_hbm, list_vm, 2), load(length_hbm, length_vm, 3), load(q_hbm, q_vm, 4),
        load(new_k_hbm, new_k_vm, 5), load(new_v_hbm, new_v_vm, 6),
    ]
    load_k, load_v = load(k_hbm, k_vm, 0), load(v_hbm, v_vm, 1)

    def after(here, step, size):
        moved = here + step
        return jnp.where(moved >= size, moved - size, moved)

    def rank_at(step):
        return after(rank, step + 1, ranks)

    shard_at = [shard] + [after(shard, step, shards) for step in range(1, shards)]

    def everyone(body):
        for other in shard_at[1:]:
            body(rank, other)

        def rank_body(step):
            there = rank_at(step)
            for other in shard_at:
                body(there, other)

        each(ranks - 1, rank_body)

    barrier = pltpu.get_barrier_semaphore()

    def greet(there, other):
        pl.semaphore_signal(
            barrier, inc=1, device_id=(there, other), device_id_type=pl.DeviceIdType.MESH
        )

    everyone(greet)

    def holders(body):
        each(ranks - 1, lambda step: body(rank_at(step)))

    lane = iota((1, LANES), 1)
    listed = list_vm.shape[2]
    entries = micro * listed
    per_row = LANES // entries
    offset = within(me, per_row) * entries
    for copy in small:
        copy.wait()
    blank = jnp.zeros((1, LANES - listed), F32)
    slot = within(lane, entries)
    pool_rows = jnp.zeros((1, LANES), F32)
    count = jnp.zeros((1, LANES), jnp.int32)
    for m in range(micro):
        listing = list_vm[m]
        pool = (listing[0:1] * slots + listing[1:2]).astype(F32)
        pool = jnp.concatenate([pool, blank], axis=1)
        pool_rows = pool_rows + (pltpu.roll(pool, m * listed, 1) if m else pool)
        position = shard * listed + slot - m * listed
        left = jnp.clip(length_vm[0:1, m : m + 1] - position * tokens, 0, tokens)
        count = jnp.where(over(slot, listed) == m, left, count)
    width = entries
    while width < LANES:
        pool_rows = pool_rows + pltpu.roll(pool_rows, width, 1)
        width *= 2
    mine = (lane >= offset) & (lane < offset + entries)
    meta_all[me, 0:1] = jnp.where(mine, pool_rows, 0.0)
    meta_all[me, 1:2] = jnp.where(mine, count.astype(F32), 0.0)
    q_wide = q_vm[0].astype(F32)
    own_q = jnp.concatenate(
        [
            q_wide[m : m + 1, n * dim : (n + 1) * dim] for m in range(micro) for n in range(heads)
        ], 0,
    )
    q_all[rank] = own_q.astype(BF16)
    pl.semaphore_wait(barrier, devices - 1)

    def send(src, dst, which, target):
        pltpu.make_async_remote_copy(
            src_ref=src, dst_ref=dst, send_sem=send_sem.at[which], recv_sem=recv_sem.at[which],
            device_id=target, device_id_type=pl.DeviceIdType.MESH,
        ).start()

    def drain(ref, sem, which, count):
        part = ref.at[pl.ds(0, count)]
        pltpu.make_async_copy(part, part, sem.at[which]).wait()

    everyone(lambda there, other: send(meta_all.at[me], meta_all.at[me], 0, (there, other)))
    holders(lambda there: send(q_all.at[rank], q_all.at[rank], 1, (there, shard)))

    row_lane = within(iota((rows, LANES), 1), rows) == iota((rows, LANES), 0)
    spread_t = over(iota((slots, tall), 1), heads) == iota((slots, tall), 0)
    ones = jnp.ones((LANES, LANES), BF16)

    def per_head(ref):
        flat = ref[0].astype(F32)
        return jnp.concatenate(
            [jnp.broadcast_to(flat[m : m + 1], (heads, dim)) for m in range(micro)], 0
        )

    own = jnp.sum(own_q * per_head(new_k_vm), axis=1, keepdims=True) * scale
    own_row = jnp.sum(jnp.where(row_lane, own, 0.0), axis=0, keepdims=True)

    drain(meta_all, recv_sem, 0, devices - 1)
    slot_row = (rank * slots + iota((slots, LANES), 0)).astype(F32)

    def find(group, carry):
        request, live = carry
        parts = meta_all[pl.ds(group * per_row, per_row)]
        both = jnp.sum(parts, axis=0)
        owner = over(group * per_row + over(lane, entries), shards)
        name = (owner * micro + over(within(lane, entries), listed)).astype(F32)
        match = jnp.broadcast_to(both[0:1], (slots, LANES)) == slot_row
        request = request + jnp.where(match, name, 0.0)
        live = live + jnp.where(match, both[1:2], 0.0)
        return request, live

    found = (jnp.zeros((slots, LANES), F32), jnp.zeros((slots, LANES), F32))
    groups = devices // per_row
    if groups < 16:
        for group in range(groups):
            found = find(group, found)
    else:
        found = lax.fori_loop(0, groups, find, found)
    summed = matmul(jnp.concatenate(found, axis=0).astype(BF16), ones)
    request = summed[:slots]
    def heads_of(values):
        return jnp.concatenate(
            [jnp.broadcast_to(values[i : i + 1], (heads, LANES)) for i in range(slots)], 0
        )

    request_tall, live_tall = heads_of(request), heads_of(summed[slots:])
    target = request_tall * heads + within(iota((tall, LANES), 0), heads).astype(F32)
    target_row = jnp.sum(
        jnp.where(spread_t, jnp.concatenate([request] * (tall // LANES), axis=1), 0.0),
        axis=0, keepdims=True,
    ) * heads + within(iota((1, tall), 1), heads).astype(F32)

    def choose(c):
        for at in range(0, chunk_rows, LANES):
            column = (c * chunk_rows + at + iota((tall, LANES), 1)).astype(F32)
            pick[c, :, at : at + LANES] = jnp.where(target == column, 1.0, 0.0).astype(BF16)
        held[c] = jnp.where(
            (c * chunk_rows + iota((chunk_rows, tall), 0)).astype(F32) == target_row, 1.0, 0.0
        ).astype(BF16)

    each_chunk = lambda body: body(0) if chunks == 1 else pl.loop(0, chunks)(body)
    each_chunk(choose)

    drain(q_all, recv_sem, 1, ranks - 1)
    if chunks == 1:
        q_sel[...] = matmul(pick[0], q_all[...].reshape(chunk_rows, dim))
    else:
        q_sel[...] = jnp.zeros((tall, dim), F32)

        @pl.loop(0, chunks)
        def _(c):
            part = q_all[pl.ds(c * RANK_CHUNK, RANK_CHUNK)].reshape(chunk_rows, dim)
            q_sel[...] += matmul(pick[c], part)

    load_k.wait()
    pairs = slots // 2
    crossed = lax.dot_general(
        q_sel[...].astype(BF16).reshape(pairs, 2 * heads, dim),
        k_vm[...].reshape(pairs, 2 * tokens, dim),
        (((2,), (2,)), ((0,), (0,))),
        preferred_element_type=F32,
    )
    raw = jnp.stack([crossed[:, :heads, :tokens], crossed[:, heads:, tokens:]], axis=1)
    raw = raw.reshape(tall, tokens) * scale
    alive = iota((tall, tokens), 1).astype(F32) < live_tall
    raw = jnp.where(alive, raw, LOW)
    peak = jnp.max(raw, axis=1, keepdims=True)
    weight = jnp.exp(raw - peak).astype(BF16)
    total = matmul(weight, ones)
    load_v.wait()
    paired = weight.reshape(pairs, 2, heads, tokens)
    nothing = jnp.zeros((pairs, heads, tokens), BF16)
    diagonal = jnp.concatenate(
        [
            jnp.concatenate([paired[:, 0], nothing], axis=2),
            jnp.concatenate([nothing, paired[:, 1]], axis=2),
        ], 1,
    )
    mixed = lax.dot_general(
        diagonal, v_vm[...].reshape(pairs, 2 * tokens, dim), (((2,), (1,)), ((0,), (0,))),
        preferred_element_type=F32,
    ).reshape(tall, dim)

    def ceilings(c):
        name = (c * RANK_CHUNK * micro + iota((tall, LANES), 1)).astype(F32)
        best = jnp.where(request_tall == name, peak, LOW).reshape(slots, heads, LANES)
        best = jnp.max(best, axis=0).astype(BF16).astype(F32)
        top = jnp.concatenate(
            [
                jnp.broadcast_to(best[:, r : r + 1], (heads, LANES))
                for r in range(RANK_CHUNK * micro)
            ], 0,
        )
        stat_rows(c, 0, top)
        return top.astype(BF16)

    lane_slot = within(rank, LANES // rows) * rows

    def stat_rows(c, which, values):
        mine = iota((rows, LANES), 1) == iota((rows, LANES), 0) + lane_slot
        for o in range(RANK_CHUNK):
            part = jnp.where(mine, values[o * rows : (o + 1) * rows], 0.0)
            stat_out[c * RANK_CHUNK + o, which : which + 1] = jnp.sum(part, axis=0, keepdims=True)

    if chunks == 1:
        ceil_rep[...] = matmul(pick[0], ceilings(0))
    else:
        ceil_rep[...] = jnp.zeros((tall, LANES), F32)

        @pl.loop(0, chunks)
        def _(c):
            ceil_rep[...] += matmul(pick[c], ceilings(c))

    rescale = jnp.exp(peak - ceil_rep[...])
    both = jnp.concatenate([(mixed * rescale).astype(BF16), (total * rescale).astype(BF16)], axis=1)

    def combine(c):
        merged = matmul(held[c], both)
        stat_rows(c, 1, merged[:, dim:])
        acc_out[pl.ds(c * RANK_CHUNK, RANK_CHUNK)] = (
            merged[:, :dim].astype(BF16).reshape(RANK_CHUNK, rows, dim)
        )

    each_chunk(combine)

    holders(lambda there: send(stat_out.at[there], stat_in.at[rank], 2, (there, shard)))
    holders(lambda there: send(acc_out.at[there], acc_in.at[rank], 3, (there, shard)))
    stat_in[rank] = stat_out[rank]
    acc_in[rank] = acc_out[rank]

    drain(stat_in, recv_sem, 2, ranks - 1)
    per_group = LANES // rows
    stats = [
        jnp.sum(stat_in[g : g + per_group], axis=0) for g in range(0, ranks, per_group)
    ]
    ceiling = own_row
    for both in stats:
        ceiling = jnp.maximum(ceiling, both[0:1])
    shift = LANES // 2
    while shift >= rows:
        ceiling = jnp.maximum(ceiling, pltpu.roll(ceiling, shift, 1))
        shift //= 2
    shares = [jnp.exp(both[0:1] - ceiling) for both in stats]
    bottom = sum(share * both[1:2] for share, both in zip(shares, stats))
    shift = LANES // 2
    while shift >= rows:
        bottom = bottom + pltpu.roll(bottom, shift, 1)
        shift //= 2
    own_share = jnp.exp(own_row - ceiling)
    inverse = 1.0 / (bottom + own_share)
    first = iota((rows, LANES), 1) == iota((rows, LANES), 0)
    own_column = jnp.sum(jnp.where(first, own_share * inverse, 0.0), axis=1, keepdims=True)
    result = own_column * per_head(new_v_vm)

    drain(acc_in, recv_sem, 3, ranks - 1)
    for g, share in enumerate(shares):
        factor = jnp.where(row_lane, share * inverse, 0.0)
        high = factor.astype(BF16)
        low = (factor - high.astype(F32)).astype(BF16)
        part = acc_in[g * per_group : (g + 1) * per_group].reshape(LANES, dim)
        result = result + matmul(high, part) + matmul(low, part)
    for n in range(heads):
        pair = [result[m * heads + n : m * heads + n + 1] for m in range(micro)]
        out_ref[0, :, n * dim : (n + 1) * dim] = jnp.concatenate(pair, axis=0).astype(BF16)

    drain(meta_all, send_sem, 0, devices - 1)
    drain(q_all, send_sem, 1, ranks - 1)
    drain(stat_out, send_sem, 2, ranks - 1)
    drain(acc_out, send_sem, 3, ranks - 1)


def per_device(
    ranks, shards, queries, new_token_keys, new_token_values, key_pool, value_pool, block_list, context_len
):
    micro, requests, width = queries.shape
    slots, tokens, dim = key_pool.shape
    heads = width // dim
    rows = micro * heads
    queries, new_token_keys, new_token_values = (
        x.transpose(1, 0, 2) for x in (queries, new_token_keys, new_token_values)
    )
    block_list, context_len = block_list.transpose(0, 2, 1), context_len.transpose(1, 0)
    tall = slots * heads
    chunks = ranks // RANK_CHUNK
    chunk_rows = RANK_CHUNK * rows
    vmem = pl.BlockSpec(memory_space=pltpu.VMEM)
    anywhere = pl.BlockSpec(memory_space=pl.ANY)
    out = pl.pallas_call(
        partial(kernel, ranks, shards, micro, heads),
        out_shape=pltpu.VMEM(queries.shape, BF16),
        in_specs=[anywhere] * 7,
        out_specs=vmem,
        scratch_shapes=[
            pltpu.VMEM(queries.shape, BF16),
            pltpu.VMEM(new_token_keys.shape, BF16),
            pltpu.VMEM(new_token_values.shape, BF16),
            pltpu.VMEM(block_list.shape, jnp.int32),
            pltpu.VMEM(context_len.shape, jnp.int32),
            pltpu.VMEM((ranks * shards, 2, LANES), F32),
            pltpu.VMEM((ranks, rows, dim), BF16),
            pltpu.VMEM((slots, tokens, dim), BF16),
            pltpu.VMEM((slots, tokens, dim), BF16),
            pltpu.VMEM((chunks, tall, chunk_rows), BF16),
            pltpu.VMEM((chunks, chunk_rows, tall), BF16),
            pltpu.VMEM((tall, dim), F32),
            pltpu.VMEM((tall, LANES), F32),
            pltpu.VMEM((ranks, rows, dim), BF16),
            pltpu.VMEM((ranks, 2, LANES), F32),
            pltpu.VMEM((ranks, rows, dim), BF16),
            pltpu.VMEM((ranks, 2, LANES), F32),
            pltpu.SemaphoreType.DMA((7,)),
            pltpu.SemaphoreType.DMA((4,)),
            pltpu.SemaphoreType.DMA((4,)),
        ],
        compiler_params=pltpu.CompilerParams(
            collective_id=0, has_side_effects=True, vmem_limit_bytes=VMEM_BYTES
        ),
        name="paged_decode",
    )(
        queries, new_token_keys, new_token_values, block_list, context_len, key_pool, value_pool
    )
    return out.transpose(1, 0, 2)


def solution(mesh):
    placed = (
        P(None, "dp", "tp"),
        P(None, "dp", "tp"),
        P(None, "dp", "tp"),
        P("dp", None, "tp"),
        P("dp", None, "tp"),
        P(None, ("dp", "tp"), None),
        P(None, "dp"),
    )
    return jax.shard_map(
        partial(per_device, mesh.shape["dp"], mesh.shape["tp"]),
        mesh=mesh, in_specs=placed, out_specs=P(None, "dp", "tp"), check_vma=False,
    )
```

```python
from functools import partial

import jax
import jax.numpy as jnp
from jax import lax
from jax.experimental import pallas as pl
from jax.experimental.pallas import tpu as pltpu
from jax.sharding import PartitionSpec as P

F32, BF16 = jnp.float32, jnp.bfloat16
LOW = -1e30
LANES = 128
RANK_CHUNK = 8
VMEM_BYTES = 56 << 20
ROLLED_FROM = 64


def each(count, body):
    if count < ROLLED_FROM:
        for index in range(count):
            body(index)
    else:
        pl.loop(0, count)(body)


def iota(shape, axis):
    return lax.broadcasted_iota(jnp.int32, shape, axis)


def over(values, size):
    if size & (size - 1):
        return values // size
    return lax.shift_right_logical(values, jnp.full_like(values, size.bit_length() - 1))


def within(values, size):
    return values - over(values, size) * size if size & (size - 1) else values & (size - 1)


def matmul(a, b):
    return jnp.dot(a, b, preferred_element_type=F32)


def kernel(
    ranks, shards, micro, heads,
    q_hbm, new_k_hbm, new_v_hbm, list_hbm, length_hbm, k_hbm, v_hbm, out_ref,
    q_vm, new_k_vm, new_v_vm, list_vm, length_vm, meta_all, q_all, k_vm, v_vm, pick, held, q_sel, ceil_rep, acc_out, stat_out,
    acc_in, stat_in, load_sem, send_sem, recv_sem,
):
    devices = ranks * shards
    slots, tokens, dim = k_vm.shape
    rows = micro * heads
    tall = slots * heads
    chunk_rows = RANK_CHUNK * rows
    chunks = ranks // RANK_CHUNK
    scale = dim ** (-0.5)
    rank, shard = lax.axis_index("dp"), lax.axis_index("tp")
    me = rank * shards + shard

    def load(src, dst, which):
        copy = pltpu.make_async_copy(src, dst, load_sem.at[which])
        copy.start()
        return copy

    small = [
        load(list_hbm, list_vm, 2), load(length_hbm, length_vm, 3), load(q_hbm, q_vm, 4),
        load(new_k_hbm, new_k_vm, 5), load(new_v_hbm, new_v_vm, 6),
    ]
    load_k, load_v = load(k_hbm, k_vm, 0), load(v_hbm, v_vm, 1)

    def after(here, step, size):
        moved = here + step
        return jnp.where(moved >= size, moved - size, moved)

    def rank_at(step):
        return after(rank, step + 1, ranks)

    shard_at = [shard] + [after(shard, step, shards) for step in range(1, shards)]

    def everyone(body):
        for other in shard_at[1:]:
            body(rank, other)

        def rank_body(step):
            there = rank_at(step)
            for other in shard_at:
                body(there, other)

        each(ranks - 1, rank_body)

    barrier = pltpu.get_barrier_semaphore()

    def greet(there, other):
        pl.semaphore_signal(
            barrier, inc=1, device_id=(there, other), device_id_type=pl.DeviceIdType.MESH
        )

    everyone(greet)

    def holders(body):
        each(ranks - 1, lambda step: body(rank_at(step)))

    lane = iota((1, LANES), 1)
    listed = list_vm.shape[2]
    entries = micro * listed
    span = 2 * entries
    per_row = LANES // span
    offset = within(me, per_row) * span
    for copy in small:
        copy.wait()
    blank = jnp.zeros((1, LANES - listed), F32)
    slot = within(lane, entries)
    pool_rows = jnp.zeros((1, LANES), F32)
    count = jnp.zeros((1, LANES), jnp.int32)
    for m in range(micro):
        listing = list_vm[m]
        pool = (listing[0:1] * slots + listing[1:2]).astype(F32)
        pool = jnp.concatenate([pool, blank], axis=1)
        pool_rows = pool_rows + (pltpu.roll(pool, m * listed, 1) if m else pool)
        position = shard * listed + slot - m * listed
        left = jnp.clip(length_vm[0:1, m : m + 1] - position * tokens, 0, tokens)
        count = jnp.where(over(slot, listed) == m, left, count)
    width = entries
    while width < LANES:
        pool_rows = pool_rows + pltpu.roll(pool_rows, width, 1)
        width *= 2
    first = within(lane, span) < entries
    mine = (lane >= offset) & (lane < offset + span)
    both = jnp.where(first, pool_rows, count.astype(F32))
    meta_all[me] = jnp.where(mine, both, 0.0)
    q_wide = q_vm[0].astype(F32)
    own_q = jnp.concatenate(
        [
            q_wide[m : m + 1, n * dim : (n + 1) * dim] for m in range(micro) for n in range(heads)
        ], 0,
    )
    q_all[rank] = own_q.astype(BF16)
    pl.semaphore_wait(barrier, devices - 1)

    def send(src, dst, which, target):
        pltpu.make_async_remote_copy(
            src_ref=src, dst_ref=dst, send_sem=send_sem.at[which], recv_sem=recv_sem.at[which],
            device_id=target, device_id_type=pl.DeviceIdType.MESH,
        ).start()

    def drain(ref, sem, which, count):
        part = ref.at[pl.ds(0, count)]
        pltpu.make_async_copy(part, part, sem.at[which]).wait()

    everyone(lambda there, other: send(meta_all.at[me], meta_all.at[me], 0, (there, other)))
    holders(lambda there: send(q_all.at[rank], q_all.at[rank], 1, (there, shard)))

    row_lane = within(iota((rows, LANES), 1), rows) == iota((rows, LANES), 0)
    spread_t = over(iota((slots, tall), 1), heads) == iota((slots, tall), 0)
    ones = jnp.ones((LANES, LANES), BF16)

    def per_head(ref):
        flat = ref[0].astype(F32)
        return jnp.concatenate(
            [jnp.broadcast_to(flat[m : m + 1], (heads, dim)) for m in range(micro)], 0
        )

    own = jnp.sum(own_q * per_head(new_k_vm), axis=1, keepdims=True) * scale
    own_row = jnp.sum(jnp.where(row_lane, own, 0.0), axis=0, keepdims=True)

    drain(meta_all, recv_sem, 0, devices - 1)
    slot_row = (rank * slots + iota((slots, LANES), 0)).astype(F32)

    def find(group, carry):
        request, live = carry
        parts = meta_all[pl.ds(group * per_row, per_row)]
        both = jnp.sum(parts, axis=0)
        owner = over(group * per_row + over(lane, span), shards)
        name = (owner * micro + over(within(lane, span), listed)).astype(F32)
        match = jnp.broadcast_to(jnp.where(first, both, -1.0), (slots, LANES)) == slot_row
        request = request + jnp.where(match, name, 0.0)
        live = live + jnp.where(match, pltpu.roll(both, LANES - entries, 1), 0.0)
        return request, live

    found = (jnp.zeros((slots, LANES), F32), jnp.zeros((slots, LANES), F32))
    groups = devices // per_row
    if groups < 16:
        for group in range(groups):
            found = find(group, found)
    else:
        found = lax.fori_loop(0, groups, find, found)
    summed = matmul(jnp.concatenate(found, axis=0).astype(BF16), ones)
    request = summed[:slots]
    def heads_of(values):
        return jnp.concatenate(
            [jnp.broadcast_to(values[i : i + 1], (heads, LANES)) for i in range(slots)], 0
        )

    request_tall, live_tall = heads_of(request), heads_of(summed[slots:])
    target = request_tall * heads + within(iota((tall, LANES), 0), heads).astype(F32)
    target_row = jnp.sum(
        jnp.where(spread_t, jnp.concatenate([request] * (tall // LANES), axis=1), 0.0),
        axis=0, keepdims=True,
    ) * heads + within(iota((1, tall), 1), heads).astype(F32)

    one, zero = jnp.ones((), BF16), jnp.zeros((), BF16)
    row_name = iota((chunk_rows, LANES), 0).astype(F32).astype(BF16)

    def choose(c):
        base = jnp.asarray(c * chunk_rows, jnp.int32).astype(F32)
        wanted = (target - base).astype(BF16)
        for at in range(0, chunk_rows, LANES):
            column = jnp.broadcast_to((lane + at).astype(F32).astype(BF16), (tall, LANES))
            pick[c, :, at : at + LANES] = jnp.where(wanted == column, one, zero)
        for at in range(0, tall, LANES):
            here = jnp.broadcast_to(target_row[:, at : at + LANES] - base, (chunk_rows, LANES))
            held[c, :, at : at + LANES] = jnp.where(here.astype(BF16) == row_name, one, zero)

    each_chunk = lambda body: body(0) if chunks == 1 else pl.loop(0, chunks)(body)
    each_chunk(choose)

    drain(q_all, recv_sem, 1, ranks - 1)
    if chunks == 1:
        q_sel[...] = matmul(pick[0], q_all[...].reshape(chunk_rows, dim))
    else:
        q_sel[...] = jnp.zeros((tall, dim), F32)

        @pl.loop(0, chunks)
        def _(c):
            part = q_all[pl.ds(c * RANK_CHUNK, RANK_CHUNK)].reshape(chunk_rows, dim)
            q_sel[...] += matmul(pick[c], part)

    load_k.wait()
    pairs = slots // 2
    crossed = lax.dot_general(
        q_sel[...].astype(BF16).reshape(pairs, 2 * heads, dim),
        k_vm[...].reshape(pairs, 2 * tokens, dim),
        (((2,), (2,)), ((0,), (0,))),
        preferred_element_type=F32,
    )
    raw = jnp.stack([crossed[:, :heads, :tokens], crossed[:, heads:, tokens:]], axis=1)
    raw = raw.reshape(tall, tokens) * scale
    alive = iota((tall, tokens), 1).astype(F32) < live_tall
    raw = jnp.where(alive, raw, LOW)
    peak = jnp.max(raw, axis=1, keepdims=True)
    weight = jnp.exp(raw - peak).astype(BF16)
    total = matmul(weight, ones)
    load_v.wait()
    paired = weight.reshape(pairs, 2, heads, tokens)
    nothing = jnp.zeros((pairs, heads, tokens), BF16)
    diagonal = jnp.concatenate(
        [
            jnp.concatenate([paired[:, 0], nothing], axis=2),
            jnp.concatenate([nothing, paired[:, 1]], axis=2),
        ], 1,
    )
    mixed = lax.dot_general(
        diagonal, v_vm[...].reshape(pairs, 2 * tokens, dim), (((2,), (1,)), ((0,), (0,))),
        preferred_element_type=F32,
    ).reshape(tall, dim)

    def ceilings(c):
        name = (c * RANK_CHUNK * micro + iota((tall, LANES), 1)).astype(F32)
        best = jnp.where(request_tall == name, peak, LOW).reshape(slots, heads, LANES)
        best = jnp.max(best, axis=0).astype(BF16).astype(F32)
        top = jnp.concatenate(
            [
                jnp.broadcast_to(best[:, r : r + 1], (heads, LANES))
                for r in range(RANK_CHUNK * micro)
            ], 0,
        )
        stat_rows(c, 0, top)
        return top.astype(BF16)

    lane_slot = within(rank, LANES // rows) * rows

    def stat_rows(c, which, values):
        mine = iota((rows, LANES), 1) == iota((rows, LANES), 0) + lane_slot
        for o in range(RANK_CHUNK):
            part = jnp.where(mine, values[o * rows : (o + 1) * rows], 0.0)
            stat_out[c * RANK_CHUNK + o, which : which + 1] = jnp.sum(part, axis=0, keepdims=True)

    if chunks == 1:
        ceil_rep[...] = matmul(pick[0], ceilings(0))
    else:
        ceil_rep[...] = jnp.zeros((tall, LANES), F32)

        @pl.loop(0, chunks)
        def _(c):
            ceil_rep[...] += matmul(pick[c], ceilings(c))

    rescale = jnp.exp(peak - ceil_rep[...])
    both = jnp.concatenate([(mixed * rescale).astype(BF16), (total * rescale).astype(BF16)], axis=1)

    def combine(c):
        merged = matmul(held[c], both)
        stat_rows(c, 1, merged[:, dim:])
        acc_out[pl.ds(c * RANK_CHUNK, RANK_CHUNK)] = (
            merged[:, :dim].astype(BF16).reshape(RANK_CHUNK, rows, dim)
        )

    each_chunk(combine)

    holders(lambda there: send(stat_out.at[there], stat_in.at[rank], 2, (there, shard)))
    holders(lambda there: send(acc_out.at[there], acc_in.at[rank], 3, (there, shard)))
    stat_in[rank] = stat_out[rank]
    acc_in[rank] = acc_out[rank]

    drain(stat_in, recv_sem, 2, ranks - 1)
    per_group = LANES // rows
    stats = [
        jnp.sum(stat_in[g : g + per_group], axis=0) for g in range(0, ranks, per_group)
    ]
    ceiling = own_row
    for both in stats:
        ceiling = jnp.maximum(ceiling, both[0:1])
    shift = LANES // 2
    while shift >= rows:
        ceiling = jnp.maximum(ceiling, pltpu.roll(ceiling, shift, 1))
        shift //= 2
    shares = [jnp.exp(both[0:1] - ceiling) for both in stats]
    bottom = sum(share * both[1:2] for share, both in zip(shares, stats))
    shift = LANES // 2
    while shift >= rows:
        bottom = bottom + pltpu.roll(bottom, shift, 1)
        shift //= 2
    own_share = jnp.exp(own_row - ceiling)
    inverse = 1.0 / (bottom + own_share)
    head_lane = iota((rows, LANES), 1) == iota((rows, LANES), 0)
    own_column = jnp.sum(jnp.where(head_lane, own_share * inverse, 0.0), axis=1, keepdims=True)
    result = own_column * per_head(new_v_vm)

    drain(acc_in, recv_sem, 3, ranks - 1)
    for g, share in enumerate(shares):
        factor = jnp.where(row_lane, share * inverse, 0.0)
        high = factor.astype(BF16)
        low = (factor - high.astype(F32)).astype(BF16)
        part = acc_in[g * per_group : (g + 1) * per_group].reshape(LANES, dim)
        result = result + matmul(high, part) + matmul(low, part)
    for n in range(heads):
        pair = [result[m * heads + n : m * heads + n + 1] for m in range(micro)]
        out_ref[0, :, n * dim : (n + 1) * dim] = jnp.concatenate(pair, axis=0).astype(BF16)

    drain(meta_all, send_sem, 0, devices - 1)
    drain(q_all, send_sem, 1, ranks - 1)
    drain(stat_out, send_sem, 2, ranks - 1)
    drain(acc_out, send_sem, 3, ranks - 1)


def per_device(
    ranks, shards, queries, new_token_keys, new_token_values, key_pool, value_pool, block_list, context_len
):
    micro, requests, width = queries.shape
    slots, tokens, dim = key_pool.shape
    heads = width // dim
    rows = micro * heads
    queries, new_token_keys, new_token_values = (
        x.transpose(1, 0, 2) for x in (queries, new_token_keys, new_token_values)
    )
    block_list, context_len = block_list.transpose(0, 2, 1), context_len.transpose(1, 0)
    tall = slots * heads
    chunks = ranks // RANK_CHUNK
    chunk_rows = RANK_CHUNK * rows
    vmem = pl.BlockSpec(memory_space=pltpu.VMEM)
    anywhere = pl.BlockSpec(memory_space=pl.ANY)
    out = pl.pallas_call(
        partial(kernel, ranks, shards, micro, heads),
        out_shape=pltpu.VMEM(queries.shape, BF16),
        in_specs=[anywhere] * 7,
        out_specs=vmem,
        scratch_shapes=[
            pltpu.VMEM(queries.shape, BF16),
            pltpu.VMEM(new_token_keys.shape, BF16),
            pltpu.VMEM(new_token_values.shape, BF16),
            pltpu.VMEM(block_list.shape, jnp.int32),
            pltpu.VMEM(context_len.shape, jnp.int32),
            pltpu.VMEM((ranks * shards, 1, LANES), F32),
            pltpu.VMEM((ranks, rows, dim), BF16),
            pltpu.VMEM((slots, tokens, dim), BF16),
            pltpu.VMEM((slots, tokens, dim), BF16),
            pltpu.VMEM((chunks, tall, chunk_rows), BF16),
            pltpu.VMEM((chunks, chunk_rows, tall), BF16),
            pltpu.VMEM((tall, dim), F32),
            pltpu.VMEM((tall, LANES), F32),
            pltpu.VMEM((ranks, rows, dim), BF16),
            pltpu.VMEM((ranks, 2, LANES), F32),
            pltpu.VMEM((ranks, rows, dim), BF16),
            pltpu.VMEM((ranks, 2, LANES), F32),
            pltpu.SemaphoreType.DMA((7,)),
            pltpu.SemaphoreType.DMA((4,)),
            pltpu.SemaphoreType.DMA((4,)),
        ],
        compiler_params=pltpu.CompilerParams(
            collective_id=0, has_side_effects=True, vmem_limit_bytes=VMEM_BYTES
        ),
        name="paged_decode",
    )(
        queries, new_token_keys, new_token_values, block_list, context_len, key_pool, value_pool
    )
    return out.transpose(1, 0, 2)


def solution(mesh):
    placed = (
        P(None, "dp", "tp"),
        P(None, "dp", "tp"),
        P(None, "dp", "tp"),
        P("dp", None, "tp"),
        P("dp", None, "tp"),
        P(None, ("dp", "tp"), None),
        P(None, "dp"),
    )
    return jax.shard_map(
        partial(per_device, mesh.shape["dp"], mesh.shape["tp"]),
        mesh=mesh, in_specs=placed, out_specs=P(None, "dp", "tp"), check_vma=False,
    )
```

```python
from functools import partial

import jax
import jax.numpy as jnp
from jax import lax
from jax.experimental import pallas as pl
from jax.experimental.pallas import tpu as pltpu
from jax.sharding import PartitionSpec as P

F32, BF16 = jnp.float32, jnp.bfloat16
LOW = -1e30
LANES = 128
RANK_CHUNK = 8
VMEM_BYTES = 56 << 20
ROLLED_FROM = 64


def each(count, body):
    if count < ROLLED_FROM:
        for index in range(count):
            body(index)
    else:
        pl.loop(0, count)(body)


def iota(shape, axis):
    return lax.broadcasted_iota(jnp.int32, shape, axis)


def over(values, size):
    if size & (size - 1):
        return values // size
    return lax.shift_right_logical(values, jnp.full_like(values, size.bit_length() - 1))


def within(values, size):
    return values - over(values, size) * size if size & (size - 1) else values & (size - 1)


def matmul(a, b):
    return jnp.dot(a, b, preferred_element_type=F32)


def kernel(
    ranks, shards, micro, heads,
    q_hbm, new_k_hbm, new_v_hbm, list_hbm, length_hbm, k_hbm, v_hbm, out_ref,
    q_vm, new_k_vm, new_v_vm, list_vm, length_vm, meta_all, q_all, k_vm, v_vm, pick, held, q_sel, ceil_rep, acc_out, stat_out,
    acc_in, stat_in, load_sem, send_sem, recv_sem,
):
    devices = ranks * shards
    slots, tokens, dim = k_vm.shape
    rows = micro * heads
    tall = slots * heads
    chunk_rows = RANK_CHUNK * rows
    chunks = ranks // RANK_CHUNK
    scale = dim ** (-0.5)
    rank, shard = lax.axis_index("dp"), lax.axis_index("tp")
    me = rank * shards + shard

    def load(src, dst, which):
        copy = pltpu.make_async_copy(src, dst, load_sem.at[which])
        copy.start()
        return copy

    small = [
        load(list_hbm, list_vm, 2), load(length_hbm, length_vm, 3), load(q_hbm, q_vm, 4),
        load(new_k_hbm, new_k_vm, 5), load(new_v_hbm, new_v_vm, 6),
    ]
    load_k, load_v = load(k_hbm, k_vm, 0), load(v_hbm, v_vm, 1)

    def after(here, step, size):
        moved = here + step
        return jnp.where(moved >= size, moved - size, moved)

    def rank_at(step):
        return after(rank, step + 1, ranks)

    shard_at = [shard] + [after(shard, step, shards) for step in range(1, shards)]

    def everyone(body):
        for other in shard_at[1:]:
            body(rank, other)

        def rank_body(step):
            there = rank_at(step)
            for other in shard_at:
                body(there, other)

        each(ranks - 1, rank_body)

    barrier = pltpu.get_barrier_semaphore()

    def greet(there, other):
        pl.semaphore_signal(
            barrier, inc=1, device_id=(there, other), device_id_type=pl.DeviceIdType.MESH
        )

    everyone(greet)

    def holders(body):
        each(ranks - 1, lambda step: body(rank_at(step)))

    lane = iota((1, LANES), 1)
    listed = list_vm.shape[2]
    entries = micro * listed
    span = 2 * entries
    per_row = LANES // span
    offset = within(me, per_row) * span
    for copy in small:
        copy.wait()
    blank = jnp.zeros((1, LANES - listed), F32)
    slot = within(lane, entries)
    pool_rows = jnp.zeros((1, LANES), F32)
    count = jnp.zeros((1, LANES), jnp.int32)
    for m in range(micro):
        listing = list_vm[m]
        pool = (listing[0:1] * slots + listing[1:2]).astype(F32)
        pool = jnp.concatenate([pool, blank], axis=1)
        pool_rows = pool_rows + (pltpu.roll(pool, m * listed, 1) if m else pool)
        position = shard * listed + slot - m * listed
        left = jnp.clip(length_vm[0:1, m : m + 1] - position * tokens, 0, tokens)
        count = jnp.where(over(slot, listed) == m, left, count)
    width = entries
    while width < LANES:
        pool_rows = pool_rows + pltpu.roll(pool_rows, width, 1)
        width *= 2
    first = within(lane, span) < entries
    mine = (lane >= offset) & (lane < offset + span)
    both = jnp.where(first, pool_rows, count.astype(F32))
    meta_all[me] = jnp.where(mine, both, 0.0)
    q_wide = q_vm[0].astype(F32)
    own_q = jnp.concatenate(
        [
            q_wide[m : m + 1, n * dim : (n + 1) * dim] for m in range(micro) for n in range(heads)
        ], 0,
    )
    q_all[rank] = own_q.astype(BF16)
    pl.semaphore_wait(barrier, devices - 1)

    def send(src, dst, which, target):
        pltpu.make_async_remote_copy(
            src_ref=src, dst_ref=dst, send_sem=send_sem.at[which], recv_sem=recv_sem.at[which],
            device_id=target, device_id_type=pl.DeviceIdType.MESH,
        ).start()

    def drain(ref, sem, which, count):
        part = ref.at[pl.ds(0, count)]
        pltpu.make_async_copy(part, part, sem.at[which]).wait()

    everyone(lambda there, other: send(meta_all.at[me], meta_all.at[me], 0, (there, other)))
    holders(lambda there: send(q_all.at[rank], q_all.at[rank], 1, (there, shard)))

    row_lane = within(iota((rows, LANES), 1), rows) == iota((rows, LANES), 0)
    spread_t = over(iota((slots, tall), 1), heads) == iota((slots, tall), 0)
    ones = jnp.ones((LANES, LANES), BF16)

    def per_head(ref):
        flat = ref[0].astype(F32)
        return jnp.concatenate(
            [jnp.broadcast_to(flat[m : m + 1], (heads, dim)) for m in range(micro)], 0
        )

    own = jnp.sum(own_q * per_head(new_k_vm), axis=1, keepdims=True) * scale
    own_row = jnp.sum(jnp.where(row_lane, own, 0.0), axis=0, keepdims=True)

    drain(meta_all, recv_sem, 0, devices - 1)
    slot_row = (rank * slots + iota((slots, LANES), 0)).astype(F32)

    def find(group, carry):
        request, live = carry
        parts = meta_all[pl.ds(group * per_row, per_row)]
        both = jnp.sum(parts, axis=0)
        owner = over(group * per_row + over(lane, span), shards)
        name = (owner * micro + over(within(lane, span), listed)).astype(F32)
        match = jnp.broadcast_to(jnp.where(first, both, -1.0), (slots, LANES)) == slot_row
        request = request + jnp.where(match, name, 0.0)
        live = live + jnp.where(match, pltpu.roll(both, LANES - entries, 1), 0.0)
        return request, live

    found = (jnp.zeros((slots, LANES), F32), jnp.zeros((slots, LANES), F32))
    groups = devices // per_row
    if groups < 16:
        for group in range(groups):
            found = find(group, found)
    else:
        found = lax.fori_loop(0, groups, find, found)
    summed = matmul(jnp.concatenate(found, axis=0).astype(BF16), ones)
    request = summed[:slots]
    def heads_of(values):
        return jnp.concatenate(
            [jnp.broadcast_to(values[i : i + 1], (heads, LANES)) for i in range(slots)], 0
        )

    request_tall, live_tall = heads_of(request), heads_of(summed[slots:])
    target = request_tall * heads + within(iota((tall, LANES), 0), heads).astype(F32)
    target_row = jnp.sum(
        jnp.where(spread_t, jnp.concatenate([request] * (tall // LANES), axis=1), 0.0),
        axis=0, keepdims=True,
    ) * heads + within(iota((1, tall), 1), heads).astype(F32)

    one, zero = jnp.ones((), BF16), jnp.zeros((), BF16)
    row_name = iota((chunk_rows, LANES), 0).astype(F32).astype(BF16)

    def choose(c):
        base = jnp.asarray(c * chunk_rows, jnp.int32).astype(F32)
        wanted = (target - base).astype(BF16)
        for at in range(0, chunk_rows, LANES):
            column = jnp.broadcast_to((lane + at).astype(F32).astype(BF16), (tall, LANES))
            pick[c, :, at : at + LANES] = jnp.where(wanted == column, one, zero)
        for at in range(0, tall, LANES):
            here = jnp.broadcast_to(target_row[:, at : at + LANES] - base, (chunk_rows, LANES))
            held[c, :, at : at + LANES] = jnp.where(here.astype(BF16) == row_name, one, zero)

    each_chunk = lambda body: body(0) if chunks == 1 else pl.loop(0, chunks)(body)
    each_chunk(choose)

    drain(q_all, recv_sem, 1, ranks - 1)
    if chunks == 1:
        q_sel[...] = matmul(pick[0], q_all[...].reshape(chunk_rows, dim))
    else:
        q_sel[...] = jnp.zeros((tall, dim), F32)

        @pl.loop(0, chunks)
        def _(c):
            part = q_all[pl.ds(c * RANK_CHUNK, RANK_CHUNK)].reshape(chunk_rows, dim)
            q_sel[...] += matmul(pick[c], part)

    load_k.wait()
    quads = slots // 4

    def placed(values):
        part = values.reshape(quads, 4, heads, LANES)
        nothing = jnp.zeros((quads, heads, LANES), BF16)
        rows_of = [(part[:, 0], nothing), (part[:, 2], nothing), (nothing, part[:, 1]), (nothing, part[:, 3])]
        return jnp.concatenate([jnp.concatenate(pair, axis=2) for pair in rows_of], axis=1)

    def square(values, order):
        part = values.reshape(quads, 4, LANES, LANES)
        block = [part[:, i] for i in order]
        upper, lower = jnp.concatenate(block[:2], axis=2), jnp.concatenate(block[2:], axis=2)
        return jnp.concatenate([upper, lower], axis=1)

    def useful(values):
        left, right = values[:, :, :LANES], values[:, :, LANES:]
        pieces = [
            left[:, :heads], left[:, 2 * heads : 3 * heads],
            right[:, heads : 2 * heads], right[:, 3 * heads :],
        ]
        return jnp.stack(pieces, axis=1).reshape(tall, LANES)

    raw = useful(
        lax.dot_general(
            placed(q_sel[...].astype(BF16)), square(k_vm[...], (0, 1, 2, 3)),
            (((2,), (2,)), ((0,), (0,))), preferred_element_type=F32,
        )
    ) * scale
    alive = iota((tall, tokens), 1).astype(F32) < live_tall
    raw = jnp.where(alive, raw, LOW)
    peak = jnp.max(raw, axis=1, keepdims=True)
    weight = jnp.exp(raw - peak).astype(BF16)
    total = matmul(weight, ones)
    load_v.wait()
    mixed = useful(
        lax.dot_general(
            placed(weight), square(v_vm[...], (0, 2, 1, 3)),
            (((2,), (1,)), ((0,), (0,))), preferred_element_type=F32,
        )
    )

    def ceilings(c):
        name = (c * RANK_CHUNK * micro + iota((tall, LANES), 1)).astype(F32)
        best = jnp.where(request_tall == name, peak, LOW).reshape(slots, heads, LANES)
        best = jnp.max(best, axis=0).astype(BF16).astype(F32)
        top = jnp.concatenate(
            [
                jnp.broadcast_to(best[:, r : r + 1], (heads, LANES))
                for r in range(RANK_CHUNK * micro)
            ], 0,
        )
        stat_rows(c, 0, top)
        return top.astype(BF16)

    lane_slot = within(rank, LANES // rows) * rows

    def stat_rows(c, which, values):
        mine = iota((rows, LANES), 1) == iota((rows, LANES), 0) + lane_slot
        for o in range(RANK_CHUNK):
            part = jnp.where(mine, values[o * rows : (o + 1) * rows], 0.0)
            stat_out[c * RANK_CHUNK + o, which : which + 1] = jnp.sum(part, axis=0, keepdims=True)

    if chunks == 1:
        ceil_rep[...] = matmul(pick[0], ceilings(0))
    else:
        ceil_rep[...] = jnp.zeros((tall, LANES), F32)

        @pl.loop(0, chunks)
        def _(c):
            ceil_rep[...] += matmul(pick[c], ceilings(c))

    rescale = jnp.exp(peak - ceil_rep[...])
    both = jnp.concatenate([(mixed * rescale).astype(BF16), (total * rescale).astype(BF16)], axis=1)

    def combine(c):
        merged = matmul(held[c], both)
        stat_rows(c, 1, merged[:, dim:])
        acc_out[pl.ds(c * RANK_CHUNK, RANK_CHUNK)] = (
            merged[:, :dim].astype(BF16).reshape(RANK_CHUNK, rows, dim)
        )

    each_chunk(combine)

    holders(lambda there: send(stat_out.at[there], stat_in.at[rank], 2, (there, shard)))
    holders(lambda there: send(acc_out.at[there], acc_in.at[rank], 3, (there, shard)))
    stat_in[rank] = stat_out[rank]
    acc_in[rank] = acc_out[rank]

    drain(stat_in, recv_sem, 2, ranks - 1)
    per_group = LANES // rows
    stats = [
        jnp.sum(stat_in[g : g + per_group], axis=0) for g in range(0, ranks, per_group)
    ]
    ceiling = own_row
    for both in stats:
        ceiling = jnp.maximum(ceiling, both[0:1])
    shift = LANES // 2
    while shift >= rows:
        ceiling = jnp.maximum(ceiling, pltpu.roll(ceiling, shift, 1))
        shift //= 2
    shares = [jnp.exp(both[0:1] - ceiling) for both in stats]
    bottom = sum(share * both[1:2] for share, both in zip(shares, stats))
    shift = LANES // 2
    while shift >= rows:
        bottom = bottom + pltpu.roll(bottom, shift, 1)
        shift //= 2
    own_share = jnp.exp(own_row - ceiling)
    inverse = 1.0 / (bottom + own_share)
    head_lane = iota((rows, LANES), 1) == iota((rows, LANES), 0)
    own_column = jnp.sum(jnp.where(head_lane, own_share * inverse, 0.0), axis=1, keepdims=True)
    result = own_column * per_head(new_v_vm)

    drain(acc_in, recv_sem, 3, ranks - 1)
    for g, share in enumerate(shares):
        factor = jnp.where(row_lane, share * inverse, 0.0)
        high = factor.astype(BF16)
        low = (factor - high.astype(F32)).astype(BF16)
        part = acc_in[g * per_group : (g + 1) * per_group].reshape(LANES, dim)
        result = result + matmul(high, part) + matmul(low, part)
    for n in range(heads):
        pair = [result[m * heads + n : m * heads + n + 1] for m in range(micro)]
        out_ref[0, :, n * dim : (n + 1) * dim] = jnp.concatenate(pair, axis=0).astype(BF16)

    drain(meta_all, send_sem, 0, devices - 1)
    drain(q_all, send_sem, 1, ranks - 1)
    drain(stat_out, send_sem, 2, ranks - 1)
    drain(acc_out, send_sem, 3, ranks - 1)


def per_device(
    ranks, shards, queries, new_token_keys, new_token_values, key_pool, value_pool, block_list, context_len
):
    micro, requests, width = queries.shape
    slots, tokens, dim = key_pool.shape
    heads = width // dim
    rows = micro * heads
    queries, new_token_keys, new_token_values = (
        x.transpose(1, 0, 2) for x in (queries, new_token_keys, new_token_values)
    )
    block_list, context_len = block_list.transpose(0, 2, 1), context_len.transpose(1, 0)
    tall = slots * heads
    chunks = ranks // RANK_CHUNK
    chunk_rows = RANK_CHUNK * rows
    vmem = pl.BlockSpec(memory_space=pltpu.VMEM)
    anywhere = pl.BlockSpec(memory_space=pl.ANY)
    out = pl.pallas_call(
        partial(kernel, ranks, shards, micro, heads),
        out_shape=pltpu.VMEM(queries.shape, BF16),
        in_specs=[anywhere] * 7,
        out_specs=vmem,
        scratch_shapes=[
            pltpu.VMEM(queries.shape, BF16),
            pltpu.VMEM(new_token_keys.shape, BF16),
            pltpu.VMEM(new_token_values.shape, BF16),
            pltpu.VMEM(block_list.shape, jnp.int32),
            pltpu.VMEM(context_len.shape, jnp.int32),
            pltpu.VMEM((ranks * shards, 1, LANES), F32),
            pltpu.VMEM((ranks, rows, dim), BF16),
            pltpu.VMEM((slots, tokens, dim), BF16),
            pltpu.VMEM((slots, tokens, dim), BF16),
            pltpu.VMEM((chunks, tall, chunk_rows), BF16),
            pltpu.VMEM((chunks, chunk_rows, tall), BF16),
            pltpu.VMEM((tall, dim), F32),
            pltpu.VMEM((tall, LANES), F32),
            pltpu.VMEM((ranks, rows, dim), BF16),
            pltpu.VMEM((ranks, 2, LANES), F32),
            pltpu.VMEM((ranks, rows, dim), BF16),
            pltpu.VMEM((ranks, 2, LANES), F32),
            pltpu.SemaphoreType.DMA((7,)),
            pltpu.SemaphoreType.DMA((4,)),
            pltpu.SemaphoreType.DMA((4,)),
        ],
        compiler_params=pltpu.CompilerParams(
            collective_id=0, has_side_effects=True, vmem_limit_bytes=VMEM_BYTES
        ),
        name="paged_decode",
    )(
        queries, new_token_keys, new_token_values, block_list, context_len, key_pool, value_pool
    )
    return out.transpose(1, 0, 2)


def solution(mesh):
    placed = (
        P(None, "dp", "tp"),
        P(None, "dp", "tp"),
        P(None, "dp", "tp"),
        P("dp", None, "tp"),
        P("dp", None, "tp"),
        P(None, ("dp", "tp"), None),
        P(None, "dp"),
    )
    return jax.shard_map(
        partial(per_device, mesh.shape["dp"], mesh.shape["tp"]),
        mesh=mesh, in_specs=placed, out_specs=P(None, "dp", "tp"), check_vma=False,
    )
```

```python
from functools import partial

import jax
import jax.numpy as jnp
from jax import lax
from jax.experimental import pallas as pl
from jax.experimental.pallas import tpu as pltpu
from jax.sharding import PartitionSpec as P

F32, BF16 = jnp.float32, jnp.bfloat16
LOW = -1e30
LANES = 128
RANK_CHUNK = 8
VMEM_BYTES = 56 << 20
ROLLED_FROM = 64


def each(count, body):
    if count < ROLLED_FROM:
        for index in range(count):
            body(index)
    else:
        pl.loop(0, count)(body)


def iota(shape, axis):
    return lax.broadcasted_iota(jnp.int32, shape, axis)


def over(values, size):
    if size & (size - 1):
        return values // size
    return lax.shift_right_logical(values, jnp.full_like(values, size.bit_length() - 1))


def within(values, size):
    return values - over(values, size) * size if size & (size - 1) else values & (size - 1)


def matmul(a, b):
    return jnp.dot(a, b, preferred_element_type=F32)


def kernel(
    ranks, shards, micro, heads,
    q_hbm, new_k_hbm, new_v_hbm, list_hbm, length_hbm, k_hbm, v_hbm, out_ref,
    q_vm, new_k_vm, new_v_vm, list_vm, length_vm, meta_all, q_all, k_vm, v_vm, pick, held, q_sel, ceil_rep, acc_out, stat_out,
    acc_in, stat_in, load_sem, send_sem, recv_sem,
):
    devices = ranks * shards
    slots, tokens, dim = k_vm.shape
    rows = micro * heads
    tall = slots * heads
    chunk_rows = RANK_CHUNK * rows
    chunks = ranks // RANK_CHUNK
    scale = dim ** (-0.5)
    rank, shard = lax.axis_index("dp"), lax.axis_index("tp")
    me = rank * shards + shard

    def load(src, dst, which):
        copy = pltpu.make_async_copy(src, dst, load_sem.at[which])
        copy.start()
        return copy

    small = [
        load(list_hbm, list_vm, 2), load(length_hbm, length_vm, 3), load(q_hbm, q_vm, 4),
        load(new_k_hbm, new_k_vm, 5), load(new_v_hbm, new_v_vm, 6),
    ]
    load_k, load_v = load(k_hbm, k_vm, 0), load(v_hbm, v_vm, 1)

    def after(here, step, size):
        moved = here + step
        return jnp.where(moved >= size, moved - size, moved)

    def rank_at(step):
        return after(rank, step + 1, ranks)

    shard_at = [shard] + [after(shard, step, shards) for step in range(1, shards)]

    def everyone(body):
        for other in shard_at[1:]:
            body(rank, other)

        def rank_body(step):
            there = rank_at(step)
            for other in shard_at:
                body(there, other)

        each(ranks - 1, rank_body)

    barrier = pltpu.get_barrier_semaphore()

    def greet(there, other):
        pl.semaphore_signal(
            barrier, inc=1, device_id=(there, other), device_id_type=pl.DeviceIdType.MESH
        )

    everyone(greet)

    def holders(body):
        each(ranks - 1, lambda step: body(rank_at(step)))

    lane = iota((1, LANES), 1)
    listed = list_vm.shape[2]
    entries = micro * listed
    span = 2 * entries
    per_row = LANES // span
    offset = within(me, per_row) * span
    for copy in small:
        copy.wait()
    blank = jnp.zeros((1, LANES - listed), F32)
    slot = within(lane, entries)
    pool_rows = jnp.zeros((1, LANES), F32)
    count = jnp.zeros((1, LANES), jnp.int32)
    for m in range(micro):
        listing = list_vm[m]
        pool = (listing[0:1] * slots + listing[1:2]).astype(F32)
        pool = jnp.concatenate([pool, blank], axis=1)
        pool_rows = pool_rows + (pltpu.roll(pool, m * listed, 1) if m else pool)
        position = shard * listed + slot - m * listed
        left = jnp.clip(length_vm[0:1, m : m + 1] - position * tokens, 0, tokens)
        count = jnp.where(over(slot, listed) == m, left, count)
    width = entries
    while width < LANES:
        pool_rows = pool_rows + pltpu.roll(pool_rows, width, 1)
        width *= 2
    first = within(lane, span) < entries
    mine = (lane >= offset) & (lane < offset + span)
    both = jnp.where(first, pool_rows, count.astype(F32))
    meta_all[me] = jnp.where(mine, both, 0.0)
    q_wide = q_vm[0].astype(F32)
    own_q = jnp.concatenate(
        [
            q_wide[m : m + 1, n * dim : (n + 1) * dim] for m in range(micro) for n in range(heads)
        ], 0,
    )
    q_all[rank] = own_q.astype(BF16)
    pl.semaphore_wait(barrier, devices - 1)

    def send(src, dst, which, target):
        pltpu.make_async_remote_copy(
            src_ref=src, dst_ref=dst, send_sem=send_sem.at[which], recv_sem=recv_sem.at[which],
            device_id=target, device_id_type=pl.DeviceIdType.MESH,
        ).start()

    def drain(ref, sem, which, count):
        part = ref.at[pl.ds(0, count)]
        pltpu.make_async_copy(part, part, sem.at[which]).wait()

    def tell(there, other):
        send(meta_all.at[me], meta_all.at[me], 0, (there, other))

    def ask(there):
        send(q_all.at[rank], q_all.at[rank], 1, (there, shard))
        for other in shard_at:
            tell(there, other)

    holders(ask)
    for other in shard_at[1:]:
        tell(rank, other)

    row_lane = within(iota((rows, LANES), 1), rows) == iota((rows, LANES), 0)
    spread_t = over(iota((slots, tall), 1), heads) == iota((slots, tall), 0)
    ones = jnp.ones((LANES, LANES), BF16)

    def per_head(ref):
        flat = ref[0].astype(F32)
        return jnp.concatenate(
            [jnp.broadcast_to(flat[m : m + 1], (heads, dim)) for m in range(micro)], 0
        )

    own = jnp.sum(own_q * per_head(new_k_vm), axis=1, keepdims=True) * scale
    own_row = jnp.sum(jnp.where(row_lane, own, 0.0), axis=0, keepdims=True)

    drain(meta_all, recv_sem, 0, devices - 1)
    slot_row = (rank * slots + iota((slots, LANES), 0)).astype(F32)

    def find(group, carry):
        request, live = carry
        parts = meta_all[pl.ds(group * per_row, per_row)]
        both = jnp.sum(parts, axis=0)
        owner = over(group * per_row + over(lane, span), shards)
        name = (owner * micro + over(within(lane, span), listed)).astype(F32)
        match = jnp.broadcast_to(jnp.where(first, both, -1.0), (slots, LANES)) == slot_row
        request = request + jnp.where(match, name, 0.0)
        live = live + jnp.where(match, pltpu.roll(both, LANES - entries, 1), 0.0)
        return request, live

    found = (jnp.zeros((slots, LANES), F32), jnp.zeros((slots, LANES), F32))
    groups = devices // per_row
    if groups < 16:
        for group in range(groups):
            found = find(group, found)
    else:
        found = lax.fori_loop(0, groups, find, found)
    summed = matmul(jnp.concatenate(found, axis=0).astype(BF16), ones)
    request = summed[:slots]
    def heads_of(values):
        return jnp.concatenate(
            [jnp.broadcast_to(values[i : i + 1], (heads, LANES)) for i in range(slots)], 0
        )

    request_tall, live_tall = heads_of(request), heads_of(summed[slots:])
    target = request_tall * heads + within(iota((tall, LANES), 0), heads).astype(F32)
    target_row = jnp.sum(
        jnp.where(spread_t, jnp.concatenate([request] * (tall // LANES), axis=1), 0.0),
        axis=0, keepdims=True,
    ) * heads + within(iota((1, tall), 1), heads).astype(F32)

    one, zero = jnp.ones((), BF16), jnp.zeros((), BF16)
    row_name = iota((chunk_rows, LANES), 0).astype(F32).astype(BF16)

    def choose(c):
        base = jnp.asarray(c * chunk_rows, jnp.int32).astype(F32)
        wanted = (target - base).astype(BF16)
        for at in range(0, chunk_rows, LANES):
            column = jnp.broadcast_to((lane + at).astype(F32).astype(BF16), (tall, LANES))
            pick[c, :, at : at + LANES] = jnp.where(wanted == column, one, zero)
        for at in range(0, tall, LANES):
            here = jnp.broadcast_to(target_row[:, at : at + LANES] - base, (chunk_rows, LANES))
            held[c, :, at : at + LANES] = jnp.where(here.astype(BF16) == row_name, one, zero)

    each_chunk = lambda body: body(0) if chunks == 1 else pl.loop(0, chunks)(body)
    each_chunk(choose)

    drain(q_all, recv_sem, 1, ranks - 1)
    if chunks == 1:
        q_sel[...] = matmul(pick[0], q_all[...].reshape(chunk_rows, dim))
    else:
        q_sel[...] = jnp.zeros((tall, dim), F32)

        @pl.loop(0, chunks)
        def _(c):
            part = q_all[pl.ds(c * RANK_CHUNK, RANK_CHUNK)].reshape(chunk_rows, dim)
            q_sel[...] += matmul(pick[c], part)

    load_k.wait()
    quads = slots // 4

    def placed(values):
        part = values.reshape(quads, 4, heads, LANES)
        nothing = jnp.zeros((quads, heads, LANES), BF16)
        rows_of = [(part[:, 0], nothing), (part[:, 2], nothing), (nothing, part[:, 1]), (nothing, part[:, 3])]
        return jnp.concatenate([jnp.concatenate(pair, axis=2) for pair in rows_of], axis=1)

    def square(values, order):
        part = values.reshape(quads, 4, LANES, LANES)
        block = [part[:, i] for i in order]
        upper, lower = jnp.concatenate(block[:2], axis=2), jnp.concatenate(block[2:], axis=2)
        return jnp.concatenate([upper, lower], axis=1)

    def useful(values):
        left, right = values[:, :, :LANES], values[:, :, LANES:]
        pieces = [
            left[:, :heads], left[:, 2 * heads : 3 * heads],
            right[:, heads : 2 * heads], right[:, 3 * heads :],
        ]
        return jnp.stack(pieces, axis=1).reshape(tall, LANES)

    raw = useful(
        lax.dot_general(
            placed(q_sel[...].astype(BF16)), square(k_vm[...], (0, 1, 2, 3)),
            (((2,), (2,)), ((0,), (0,))), preferred_element_type=F32,
        )
    ) * scale
    alive = iota((tall, tokens), 1).astype(F32) < live_tall
    raw = jnp.where(alive, raw, LOW)
    peak = jnp.max(raw, axis=1, keepdims=True)
    weight = jnp.exp(raw - peak).astype(BF16)
    total = matmul(weight, ones)
    load_v.wait()
    mixed = useful(
        lax.dot_general(
            placed(weight), square(v_vm[...], (0, 2, 1, 3)),
            (((2,), (1,)), ((0,), (0,))), preferred_element_type=F32,
        )
    )

    def ceilings(c):
        name = (c * RANK_CHUNK * micro + iota((tall, LANES), 1)).astype(F32)
        best = jnp.where(request_tall == name, peak, LOW).reshape(slots, heads, LANES)
        best = jnp.max(best, axis=0).astype(BF16).astype(F32)
        top = jnp.concatenate(
            [
                jnp.broadcast_to(best[:, r : r + 1], (heads, LANES))
                for r in range(RANK_CHUNK * micro)
            ], 0,
        )
        stat_rows(c, 0, top)
        return top.astype(BF16)

    lane_slot = within(rank, LANES // rows) * rows

    def stat_rows(c, which, values):
        mine = iota((rows, LANES), 1) == iota((rows, LANES), 0) + lane_slot
        for o in range(RANK_CHUNK):
            part = jnp.where(mine, values[o * rows : (o + 1) * rows], 0.0)
            stat_out[c * RANK_CHUNK + o, which : which + 1] = jnp.sum(part, axis=0, keepdims=True)

    if chunks == 1:
        ceil_rep[...] = matmul(pick[0], ceilings(0))
    else:
        ceil_rep[...] = jnp.zeros((tall, LANES), F32)

        @pl.loop(0, chunks)
        def _(c):
            ceil_rep[...] += matmul(pick[c], ceilings(c))

    rescale = jnp.exp(peak - ceil_rep[...])
    both = jnp.concatenate([(mixed * rescale).astype(BF16), (total * rescale).astype(BF16)], axis=1)

    def combine(c):
        merged = matmul(held[c], both)
        stat_rows(c, 1, merged[:, dim:])
        acc_out[pl.ds(c * RANK_CHUNK, RANK_CHUNK)] = (
            merged[:, :dim].astype(BF16).reshape(RANK_CHUNK, rows, dim)
        )

    each_chunk(combine)

    def answer(there):
        send(stat_out.at[there], stat_in.at[rank], 2, (there, shard))
        send(acc_out.at[there], acc_in.at[rank], 3, (there, shard))

    holders(answer)
    stat_in[rank] = stat_out[rank]
    acc_in[rank] = acc_out[rank]

    drain(stat_in, recv_sem, 2, ranks - 1)
    per_group = LANES // rows
    stats = [
        jnp.sum(stat_in[g : g + per_group], axis=0) for g in range(0, ranks, per_group)
    ]
    ceiling = own_row
    for both in stats:
        ceiling = jnp.maximum(ceiling, both[0:1])
    shift = LANES // 2
    while shift >= rows:
        ceiling = jnp.maximum(ceiling, pltpu.roll(ceiling, shift, 1))
        shift //= 2
    shares = [jnp.exp(both[0:1] - ceiling) for both in stats]
    bottom = sum(share * both[1:2] for share, both in zip(shares, stats))
    shift = LANES // 2
    while shift >= rows:
        bottom = bottom + pltpu.roll(bottom, shift, 1)
        shift //= 2
    own_share = jnp.exp(own_row - ceiling)
    inverse = 1.0 / (bottom + own_share)
    head_lane = iota((rows, LANES), 1) == iota((rows, LANES), 0)
    own_column = jnp.sum(jnp.where(head_lane, own_share * inverse, 0.0), axis=1, keepdims=True)
    result = own_column * per_head(new_v_vm)

    drain(acc_in, recv_sem, 3, ranks - 1)
    for g, share in enumerate(shares):
        factor = jnp.where(row_lane, share * inverse, 0.0)
        high = factor.astype(BF16)
        low = (factor - high.astype(F32)).astype(BF16)
        part = acc_in[g * per_group : (g + 1) * per_group].reshape(LANES, dim)
        result = result + matmul(high, part) + matmul(low, part)
    for n in range(heads):
        pair = [result[m * heads + n : m * heads + n + 1] for m in range(micro)]
        out_ref[0, :, n * dim : (n + 1) * dim] = jnp.concatenate(pair, axis=0).astype(BF16)

    drain(meta_all, send_sem, 0, devices - 1)
    drain(q_all, send_sem, 1, ranks - 1)
    drain(stat_out, send_sem, 2, ranks - 1)
    drain(acc_out, send_sem, 3, ranks - 1)


def per_device(
    ranks, shards, queries, new_token_keys, new_token_values, key_pool, value_pool, block_list, context_len
):
    micro, requests, width = queries.shape
    slots, tokens, dim = key_pool.shape
    heads = width // dim
    rows = micro * heads
    queries, new_token_keys, new_token_values = (
        x.transpose(1, 0, 2) for x in (queries, new_token_keys, new_token_values)
    )
    block_list, context_len = block_list.transpose(0, 2, 1), context_len.transpose(1, 0)
    tall = slots * heads
    chunks = ranks // RANK_CHUNK
    chunk_rows = RANK_CHUNK * rows
    vmem = pl.BlockSpec(memory_space=pltpu.VMEM)
    anywhere = pl.BlockSpec(memory_space=pl.ANY)
    out = pl.pallas_call(
        partial(kernel, ranks, shards, micro, heads),
        out_shape=pltpu.VMEM(queries.shape, BF16),
        in_specs=[anywhere] * 7,
        out_specs=vmem,
        scratch_shapes=[
            pltpu.VMEM(queries.shape, BF16),
            pltpu.VMEM(new_token_keys.shape, BF16),
            pltpu.VMEM(new_token_values.shape, BF16),
            pltpu.VMEM(block_list.shape, jnp.int32),
            pltpu.VMEM(context_len.shape, jnp.int32),
            pltpu.VMEM((ranks * shards, 1, LANES), F32),
            pltpu.VMEM((ranks, rows, dim), BF16),
            pltpu.VMEM((slots, tokens, dim), BF16),
            pltpu.VMEM((slots, tokens, dim), BF16),
            pltpu.VMEM((chunks, tall, chunk_rows), BF16),
            pltpu.VMEM((chunks, chunk_rows, tall), BF16),
            pltpu.VMEM((tall, dim), F32),
            pltpu.VMEM((tall, LANES), F32),
            pltpu.VMEM((ranks, rows, dim), BF16),
            pltpu.VMEM((ranks, 2, LANES), F32),
            pltpu.VMEM((ranks, rows, dim), BF16),
            pltpu.VMEM((ranks, 2, LANES), F32),
            pltpu.SemaphoreType.DMA((7,)),
            pltpu.SemaphoreType.DMA((4,)),
            pltpu.SemaphoreType.DMA((4,)),
        ],
        compiler_params=pltpu.CompilerParams(
            collective_id=0, has_side_effects=True, vmem_limit_bytes=VMEM_BYTES
        ),
        name="paged_decode",
    )(
        queries, new_token_keys, new_token_values, block_list, context_len, key_pool, value_pool
    )
    return out.transpose(1, 0, 2)


def solution(mesh):
    placed = (
        P(None, "dp", "tp"),
        P(None, "dp", "tp"),
        P(None, "dp", "tp"),
        P("dp", None, "tp"),
        P("dp", None, "tp"),
        P(None, ("dp", "tp"), None),
        P(None, "dp"),
    )
    return jax.shard_map(
        partial(per_device, mesh.shape["dp"], mesh.shape["tp"]),
        mesh=mesh, in_specs=placed, out_specs=P(None, "dp", "tp"), check_vma=False,
    )
```

```python
from functools import partial

import jax
import jax.numpy as jnp
from jax import lax
from jax.experimental import pallas as pl
from jax.experimental.pallas import tpu as pltpu
from jax.sharding import PartitionSpec as P

F32, BF16 = jnp.float32, jnp.bfloat16
LOW = -1e30
LANES = 128
RANK_CHUNK = 8
VMEM_BYTES = 56 << 20
ROLLED_FROM = 64


def each(count, body):
    if count < ROLLED_FROM:
        for index in range(count):
            body(index)
    else:
        pl.loop(0, count)(body)


def iota(shape, axis):
    return lax.broadcasted_iota(jnp.int32, shape, axis)


def over(values, size):
    if size & (size - 1):
        return values // size
    return lax.shift_right_logical(values, jnp.full_like(values, size.bit_length() - 1))


def within(values, size):
    return values - over(values, size) * size if size & (size - 1) else values & (size - 1)


def matmul(a, b):
    return jnp.dot(a, b, preferred_element_type=F32)


def kernel(
    ranks, shards, micro, heads,
    q_hbm, new_k_hbm, new_v_hbm, list_hbm, length_hbm, k_hbm, v_hbm, out_ref,
    q_vm, new_k_vm, new_v_vm, list_vm, length_vm, meta_all, q_all, k_vm, v_vm, pick, held, q_sel, ceil_rep, acc_out, stat_out,
    acc_in, stat_in, load_sem, send_sem, recv_sem,
):
    devices = ranks * shards
    slots, tokens, dim = k_vm.shape
    rows = micro * heads
    tall = slots * heads
    chunk_rows = RANK_CHUNK * rows
    chunks = ranks // RANK_CHUNK
    scale = dim ** (-0.5)
    rank, shard = lax.axis_index("dp"), lax.axis_index("tp")
    me = rank * shards + shard

    def load(src, dst, which):
        copy = pltpu.make_async_copy(src, dst, load_sem.at[which])
        copy.start()
        return copy

    small = [
        load(list_hbm, list_vm, 2), load(length_hbm, length_vm, 3), load(q_hbm, q_vm, 4),
        load(new_k_hbm, new_k_vm, 5), load(new_v_hbm, new_v_vm, 6),
    ]
    load_k, load_v = load(k_hbm, k_vm, 0), load(v_hbm, v_vm, 1)

    def after(here, step, size):
        moved = here + step
        return jnp.where(moved >= size, moved - size, moved)

    def rank_at(step):
        return after(rank, step + 1, ranks)

    shard_at = [shard] + [after(shard, step, shards) for step in range(1, shards)]

    def everyone(body):
        for other in shard_at[1:]:
            body(rank, other)

        def rank_body(step):
            there = rank_at(step)
            for other in shard_at:
                body(there, other)

        each(ranks - 1, rank_body)

    barrier = pltpu.get_barrier_semaphore()

    def greet(there, other):
        pl.semaphore_signal(
            barrier, inc=1, device_id=(there, other), device_id_type=pl.DeviceIdType.MESH
        )

    everyone(greet)

    def holders(body):
        if ranks < ROLLED_FROM:
            for step in sorted(range(ranks - 1), key=lambda i: abs(i + 1 - ranks // 2)):
                body(rank_at(step))
        else:
            each(ranks - 1, lambda step: body(rank_at(step)))

    lane = iota((1, LANES), 1)
    listed = list_vm.shape[2]
    entries = micro * listed
    span = 2 * entries
    per_row = LANES // span
    offset = within(me, per_row) * span
    for copy in small:
        copy.wait()
    blank = jnp.zeros((1, LANES - listed), F32)
    slot = within(lane, entries)
    pool_rows = jnp.zeros((1, LANES), F32)
    count = jnp.zeros((1, LANES), jnp.int32)
    for m in range(micro):
        listing = list_vm[m]
        pool = (listing[0:1] * slots + listing[1:2]).astype(F32)
        pool = jnp.concatenate([pool, blank], axis=1)
        pool_rows = pool_rows + (pltpu.roll(pool, m * listed, 1) if m else pool)
        position = shard * listed + slot - m * listed
        left = jnp.clip(length_vm[0:1, m : m + 1] - position * tokens, 0, tokens)
        count = jnp.where(over(slot, listed) == m, left, count)
    width = entries
    while width < LANES:
        pool_rows = pool_rows + pltpu.roll(pool_rows, width, 1)
        width *= 2
    first = within(lane, span) < entries
    mine = (lane >= offset) & (lane < offset + span)
    both = jnp.where(first, pool_rows, count.astype(F32))
    meta_all[me] = jnp.where(mine, both, 0.0)
    q_wide = q_vm[0].astype(F32)
    own_q = jnp.concatenate(
        [
            q_wide[m : m + 1, n * dim : (n + 1) * dim] for m in range(micro) for n in range(heads)
        ], 0,
    )
    q_all[rank] = own_q.astype(BF16)
    pl.semaphore_wait(barrier, devices - 1)

    def send(src, dst, which, target):
        pltpu.make_async_remote_copy(
            src_ref=src, dst_ref=dst, send_sem=send_sem.at[which], recv_sem=recv_sem.at[which],
            device_id=target, device_id_type=pl.DeviceIdType.MESH,
        ).start()

    def drain(ref, sem, which, count):
        part = ref.at[pl.ds(0, count)]
        pltpu.make_async_copy(part, part, sem.at[which]).wait()

    everyone(lambda there, other: send(meta_all.at[me], meta_all.at[me], 0, (there, other)))
    holders(lambda there: send(q_all.at[rank], q_all.at[rank], 1, (there, shard)))

    row_lane = within(iota((rows, LANES), 1), rows) == iota((rows, LANES), 0)
    spread_t = over(iota((slots, tall), 1), heads) == iota((slots, tall), 0)
    ones = jnp.ones((LANES, LANES), BF16)

    def per_head(ref):
        flat = ref[0].astype(F32)
        return jnp.concatenate(
            [jnp.broadcast_to(flat[m : m + 1], (heads, dim)) for m in range(micro)], 0
        )

    own = jnp.sum(own_q * per_head(new_k_vm), axis=1, keepdims=True) * scale
    own_row = jnp.sum(jnp.where(row_lane, own, 0.0), axis=0, keepdims=True)

    drain(meta_all, recv_sem, 0, devices - 1)
    slot_row = (rank * slots + iota((slots, LANES), 0)).astype(F32)

    def find(group, carry):
        request, live = carry
        parts = meta_all[pl.ds(group * per_row, per_row)]
        both = jnp.sum(parts, axis=0)
        owner = over(group * per_row + over(lane, span), shards)
        name = (owner * micro + over(within(lane, span), listed)).astype(F32)
        match = jnp.broadcast_to(jnp.where(first, both, -1.0), (slots, LANES)) == slot_row
        request = request + jnp.where(match, name, 0.0)
        live = live + jnp.where(match, pltpu.roll(both, LANES - entries, 1), 0.0)
        return request, live

    found = (jnp.zeros((slots, LANES), F32), jnp.zeros((slots, LANES), F32))
    groups = devices // per_row
    if groups < 16:
        for group in range(groups):
            found = find(group, found)
    else:
        found = lax.fori_loop(0, groups, find, found)
    summed = matmul(jnp.concatenate(found, axis=0).astype(BF16), ones)
    request = summed[:slots]
    def heads_of(values):
        return jnp.concatenate(
            [jnp.broadcast_to(values[i : i + 1], (heads, LANES)) for i in range(slots)], 0
        )

    request_tall, live_tall = heads_of(request), heads_of(summed[slots:])
    target = request_tall * heads + within(iota((tall, LANES), 0), heads).astype(F32)
    target_row = jnp.sum(
        jnp.where(spread_t, jnp.concatenate([request] * (tall // LANES), axis=1), 0.0),
        axis=0, keepdims=True,
    ) * heads + within(iota((1, tall), 1), heads).astype(F32)

    one, zero = jnp.ones((), BF16), jnp.zeros((), BF16)
    row_name = iota((chunk_rows, LANES), 0).astype(F32).astype(BF16)

    def choose(c):
        base = jnp.asarray(c * chunk_rows, jnp.int32).astype(F32)
        wanted = (target - base).astype(BF16)
        for at in range(0, chunk_rows, LANES):
            column = jnp.broadcast_to((lane + at).astype(F32).astype(BF16), (tall, LANES))
            pick[c, :, at : at + LANES] = jnp.where(wanted == column, one, zero)
        for at in range(0, tall, LANES):
            here = jnp.broadcast_to(target_row[:, at : at + LANES] - base, (chunk_rows, LANES))
            held[c, :, at : at + LANES] = jnp.where(here.astype(BF16) == row_name, one, zero)

    each_chunk = lambda body: body(0) if chunks == 1 else pl.loop(0, chunks)(body)
    each_chunk(choose)

    drain(q_all, recv_sem, 1, ranks - 1)
    if chunks == 1:
        q_sel[...] = matmul(pick[0], q_all[...].reshape(chunk_rows, dim))
    else:
        q_sel[...] = jnp.zeros((tall, dim), F32)

        @pl.loop(0, chunks)
        def _(c):
            part = q_all[pl.ds(c * RANK_CHUNK, RANK_CHUNK)].reshape(chunk_rows, dim)
            q_sel[...] += matmul(pick[c], part)

    load_k.wait()
    quads = slots // 4

    def placed(values):
        part = values.reshape(quads, 4, heads, LANES)
        nothing = jnp.zeros((quads, heads, LANES), BF16)
        rows_of = [(part[:, 0], nothing), (part[:, 2], nothing), (nothing, part[:, 1]), (nothing, part[:, 3])]
        return jnp.concatenate([jnp.concatenate(pair, axis=2) for pair in rows_of], axis=1)

    def square(values, order):
        part = values.reshape(quads, 4, LANES, LANES)
        block = [part[:, i] for i in order]
        upper, lower = jnp.concatenate(block[:2], axis=2), jnp.concatenate(block[2:], axis=2)
        return jnp.concatenate([upper, lower], axis=1)

    def useful(values):
        left, right = values[:, :, :LANES], values[:, :, LANES:]
        pieces = [
            left[:, :heads], left[:, 2 * heads : 3 * heads],
            right[:, heads : 2 * heads], right[:, 3 * heads :],
        ]
        return jnp.stack(pieces, axis=1).reshape(tall, LANES)

    raw = useful(
        lax.dot_general(
            placed(q_sel[...].astype(BF16)), square(k_vm[...], (0, 1, 2, 3)),
            (((2,), (2,)), ((0,), (0,))), preferred_element_type=F32,
        )
    ) * scale
    alive = iota((tall, tokens), 1).astype(F32) < live_tall
    raw = jnp.where(alive, raw, LOW)
    peak = jnp.max(raw, axis=1, keepdims=True)
    weight = jnp.exp(raw - peak).astype(BF16)
    total = matmul(weight, ones)
    load_v.wait()
    mixed = useful(
        lax.dot_general(
            placed(weight), square(v_vm[...], (0, 2, 1, 3)),
            (((2,), (1,)), ((0,), (0,))), preferred_element_type=F32,
        )
    )

    def ceilings(c):
        name = (c * RANK_CHUNK * micro + iota((tall, LANES), 1)).astype(F32)
        best = jnp.where(request_tall == name, peak, LOW).reshape(slots, heads, LANES)
        best = jnp.max(best, axis=0).astype(BF16).astype(F32)
        top = jnp.concatenate(
            [
                jnp.broadcast_to(best[:, r : r + 1], (heads, LANES))
                for r in range(RANK_CHUNK * micro)
            ], 0,
        )
        stat_rows(c, 0, top)
        return top.astype(BF16)

    lane_slot = within(rank, LANES // rows) * rows

    def stat_rows(c, which, values):
        mine = iota((rows, LANES), 1) == iota((rows, LANES), 0) + lane_slot
        for o in range(RANK_CHUNK):
            part = jnp.where(mine, values[o * rows : (o + 1) * rows], 0.0)
            stat_out[c * RANK_CHUNK + o, which : which + 1] = jnp.sum(part, axis=0, keepdims=True)

    if chunks == 1:
        ceil_rep[...] = matmul(pick[0], ceilings(0))
    else:
        ceil_rep[...] = jnp.zeros((tall, LANES), F32)

        @pl.loop(0, chunks)
        def _(c):
            ceil_rep[...] += matmul(pick[c], ceilings(c))

    rescale = jnp.exp(peak - ceil_rep[...])
    both = jnp.concatenate([(mixed * rescale).astype(BF16), (total * rescale).astype(BF16)], axis=1)

    def combine(c):
        merged = matmul(held[c], both)
        stat_rows(c, 1, merged[:, dim:])
        acc_out[pl.ds(c * RANK_CHUNK, RANK_CHUNK)] = (
            merged[:, :dim].astype(BF16).reshape(RANK_CHUNK, rows, dim)
        )

    each_chunk(combine)

    holders(lambda there: send(stat_out.at[there], stat_in.at[rank], 2, (there, shard)))
    holders(lambda there: send(acc_out.at[there], acc_in.at[rank], 3, (there, shard)))
    stat_in[rank] = stat_out[rank]
    acc_in[rank] = acc_out[rank]

    drain(stat_in, recv_sem, 2, ranks - 1)
    per_group = LANES // rows
    stats = [
        jnp.sum(stat_in[g : g + per_group], axis=0) for g in range(0, ranks, per_group)
    ]
    ceiling = own_row
    for both in stats:
        ceiling = jnp.maximum(ceiling, both[0:1])
    shift = LANES // 2
    while shift >= rows:
        ceiling = jnp.maximum(ceiling, pltpu.roll(ceiling, shift, 1))
        shift //= 2
    shares = [jnp.exp(both[0:1] - ceiling) for both in stats]
    bottom = sum(share * both[1:2] for share, both in zip(shares, stats))
    shift = LANES // 2
    while shift >= rows:
        bottom = bottom + pltpu.roll(bottom, shift, 1)
        shift //= 2
    own_share = jnp.exp(own_row - ceiling)
    inverse = 1.0 / (bottom + own_share)
    head_lane = iota((rows, LANES), 1) == iota((rows, LANES), 0)
    own_column = jnp.sum(jnp.where(head_lane, own_share * inverse, 0.0), axis=1, keepdims=True)
    result = own_column * per_head(new_v_vm)

    drain(acc_in, recv_sem, 3, ranks - 1)
    for g, share in enumerate(shares):
        factor = jnp.where(row_lane, share * inverse, 0.0)
        high = factor.astype(BF16)
        low = (factor - high.astype(F32)).astype(BF16)
        part = acc_in[g * per_group : (g + 1) * per_group].reshape(LANES, dim)
        result = result + matmul(high, part) + matmul(low, part)
    for n in range(heads):
        pair = [result[m * heads + n : m * heads + n + 1] for m in range(micro)]
        out_ref[0, :, n * dim : (n + 1) * dim] = jnp.concatenate(pair, axis=0).astype(BF16)

    drain(meta_all, send_sem, 0, devices - 1)
    drain(q_all, send_sem, 1, ranks - 1)
    drain(stat_out, send_sem, 2, ranks - 1)
    drain(acc_out, send_sem, 3, ranks - 1)


def per_device(
    ranks, shards, queries, new_token_keys, new_token_values, key_pool, value_pool, block_list, context_len
):
    micro, requests, width = queries.shape
    slots, tokens, dim = key_pool.shape
    heads = width // dim
    rows = micro * heads
    queries, new_token_keys, new_token_values = (
        x.transpose(1, 0, 2) for x in (queries, new_token_keys, new_token_values)
    )
    block_list, context_len = block_list.transpose(0, 2, 1), context_len.transpose(1, 0)
    tall = slots * heads
    chunks = ranks // RANK_CHUNK
    chunk_rows = RANK_CHUNK * rows
    vmem = pl.BlockSpec(memory_space=pltpu.VMEM)
    anywhere = pl.BlockSpec(memory_space=pl.ANY)
    out = pl.pallas_call(
        partial(kernel, ranks, shards, micro, heads),
        out_shape=pltpu.VMEM(queries.shape, BF16),
        in_specs=[anywhere] * 7,
        out_specs=vmem,
        scratch_shapes=[
            pltpu.VMEM(queries.shape, BF16),
            pltpu.VMEM(new_token_keys.shape, BF16),
            pltpu.VMEM(new_token_values.shape, BF16),
            pltpu.VMEM(block_list.shape, jnp.int32),
            pltpu.VMEM(context_len.shape, jnp.int32),
            pltpu.VMEM((ranks * shards, 1, LANES), F32),
            pltpu.VMEM((ranks, rows, dim), BF16),
            pltpu.VMEM((slots, tokens, dim), BF16),
            pltpu.VMEM((slots, tokens, dim), BF16),
            pltpu.VMEM((chunks, tall, chunk_rows), BF16),
            pltpu.VMEM((chunks, chunk_rows, tall), BF16),
            pltpu.VMEM((tall, dim), F32),
            pltpu.VMEM((tall, LANES), F32),
            pltpu.VMEM((ranks, rows, dim), BF16),
            pltpu.VMEM((ranks, 2, LANES), F32),
            pltpu.VMEM((ranks, rows, dim), BF16),
            pltpu.VMEM((ranks, 2, LANES), F32),
            pltpu.SemaphoreType.DMA((7,)),
            pltpu.SemaphoreType.DMA((4,)),
            pltpu.SemaphoreType.DMA((4,)),
        ],
        compiler_params=pltpu.CompilerParams(
            collective_id=0, has_side_effects=True, vmem_limit_bytes=VMEM_BYTES
        ),
        name="paged_decode",
    )(
        queries, new_token_keys, new_token_values, block_list, context_len, key_pool, value_pool
    )
    return out.transpose(1, 0, 2)


def solution(mesh):
    placed = (
        P(None, "dp", "tp"),
        P(None, "dp", "tp"),
        P(None, "dp", "tp"),
        P("dp", None, "tp"),
        P("dp", None, "tp"),
        P(None, ("dp", "tp"), None),
        P(None, "dp"),
    )
    return jax.shard_map(
        partial(per_device, mesh.shape["dp"], mesh.shape["tp"]),
        mesh=mesh, in_specs=placed, out_specs=P(None, "dp", "tp"), check_vma=False,
    )
```
